128 devices in a mesh: dp: 32 (over z, x, y_lo), expert: 4 (over y_hi, core).
Axes of the slice: x: 4, y: 4 (y_hi: 2, y_lo: 2; y = y_hi * 2 + y_lo), z: 4, core: 2. Of those that a mesh axis runs over, the one named last changes fastest.
Arguments:
- tokens: bfloat16 [65536, 2048], P(('dp', 'expert')), may hold values from -6 to 6
- out_grad: bfloat16 [65536, 2048], P(('dp', 'expert')), may hold values from -6 to 6
- chosen: int32 [4, 1024], replicated, may hold values from 0 to 65535, as said below
- slot_weight: float32 [4, 1024], P('expert'), may hold values from 0.05 to 1
- w_gate: bfloat16 [4, 2048, 1408], P('expert'), may hold values from -0.125 to 0.125
- w_up: bfloat16 [4, 2048, 1408], P('expert'), may hold values from -0.125 to 0.125
- w_down: bfloat16 [4, 1408, 2048], P('expert'), may hold values from -0.15625 to 0.15625
Outputs:
- token_grad: bfloat16 [65536, 2048], P(('dp', 'expert'))
- grad_gate: bfloat16 [4, 2048, 1408], P('expert', 'dp')
- grad_up: bfloat16 [4, 2048, 1408], P('expert', 'dp')
- grad_down: bfloat16 [4, 1408, 2048], P('expert', 'dp')
The draws below stay inside these ranges and needn't reach their ends.
Inputs may be any that keep to these rules, and one draw needn't show every extreme that they name: `chosen`: the tokens of device q, counted with dp before expert, are positions q * 512 to (q + 1) * 512 - 1; token group g is the 4 devices with dp index g. The entries of one expert's list are distinct; at most 16 of them lie on one device, and in every list there is a token group each of whose devices holds exactly 16 of them.
All inputs are finite; a program needn't handle non-finite values.
Results may differ from the reference program's by a relative error of at most 0.03.
Values may be sent and summed in bfloat16 or wider, within the bound.
A program may use at most 192 MiB of HBM per device.

```python
import math
import jax
import jax.numpy as jnp
from jax import lax

D = 2048
H = 1408
TOK_DEV = 512
EXPERTS = 4
GROUP = 2048
TOKENS = 65536
CAP = 1024
MOST = 16
ROWS = 64
N_DP = 32
N_EXPERT = 4
DEVICES = 128


def device_pick(single_key):
    return jax.random.permutation(single_key, TOK_DEV)[:MOST].astype(jnp.int32)


def expert_list(single_key):
    key_order, key_split, key_pick, key_rank = jax.random.split(single_key, 4)
    order = jax.random.permutation(key_order, N_DP)
    shares = jax.random.randint(key_split, (N_DP // 2, N_EXPERT), 0, MOST + 1)
    shares = shares.at[0].set(MOST)
    group_counts = jnp.zeros((N_DP, N_EXPERT), jnp.int32).at[order[0::2]].set(shares).at[order[1::2]].set(MOST - shares)
    device_counts = group_counts.reshape(DEVICES)
    local_rows = jax.vmap(device_pick)(jax.random.split(key_pick, DEVICES))
    positions = local_rows + (jnp.arange(DEVICES, dtype=jnp.int32) * TOK_DEV)[:, None]
    valid = jnp.arange(MOST, dtype=jnp.int32)[None, :] < device_counts[:, None]
    ranks = jax.random.permutation(key_rank, DEVICES * MOST)
    score = jnp.where(valid.reshape(-1), 0, DEVICES * MOST) + ranks
    taken = jnp.argsort(score)[:CAP]
    return positions.reshape(-1)[taken].astype(jnp.int32)


def draw_chosen(key, part):
    key = jax.random.fold_in(key, 7)
    return jax.vmap(expert_list)(jax.random.split(key, EXPERTS))


def level_of(own_key, extent, cuts, smallest, high):
    gain = 1.0
    for axis_at, shards_of in cuts:
        steps = jax.random.uniform(jax.random.fold_in(jax.random.fold_in(own_key, 6), axis_at), (shards_of,), jnp.float32, smallest / len(cuts), high / len(cuts))
        gain = gain * jnp.repeat(jnp.exp(steps), extent[axis_at] // shards_of).reshape((-1,) + (1,) * (len(extent) - 1 - axis_at))
    return gain


def normal_values(rng, extent, scale, most, shards=(), kind=jnp.bfloat16):
    values = jax.random.normal(rng, extent, jnp.float32) * scale
    if len(shards) > 0:
        values = level_of(rng, extent, shards, -0.22, 0.18) * values
    return jnp.clip(values, min=-most, max=most).astype(kind)


def setup_inputs(seed: int = 0) -> dict:
    splits = jax.random.split(jax.random.key(seed), 8)
    return {
        "tokens": normal_values(splits[0], (TOKENS, D), 1.0, 6.0, ((0, 128),)),
        "out_grad": normal_values(splits[1], (TOKENS, D), 1.0, 6.0, ((0, 128),)),
        "chosen": draw_chosen(jax.random.fold_in(splits[7], 71), 0),
        "slot_weight": jnp.clip(jnp.exp(math.log(1.0) - 2.9957323 * jax.random.uniform(splits[3], (EXPERTS, CAP), jnp.float32) ** level_of(splits[3], (EXPERTS, CAP), ((0, 4),), -0.2, 0.2)), 0.05, 1.0),
        "w_gate": normal_values(splits[4], (EXPERTS, D, H), D ** -0.5, 0.125, ((0, 4),)),
        "w_up": normal_values(splits[5], (EXPERTS, D, H), D ** -0.5, 0.125, ((0, 4),)),
        "w_down": normal_values(splits[6], (EXPERTS, H, D), H ** -0.5, 0.15625, ((0, 4),)),
    }


def slot_ranks(live, limit):
    running = jnp.cumsum(live.astype(jnp.int32), axis=1)
    wanted = jnp.arange(limit, dtype=jnp.int32)
    picked = jnp.sum((running[:, None, :] < (wanted + 1)[None, :, None]).astype(jnp.int32), axis=2)
    present = wanted[None, :] < running[:, -1:]
    return jnp.minimum(picked, live.shape[1] - 1).astype(jnp.int32), present


def rounded(part):
    return lax.optimization_barrier(part.astype(jnp.bfloat16)).astype(jnp.float32)


def expert_pass(slot_rows, slot_grads, weights, gate_matrix, up_matrix, down_matrix):
    gate_pre = jnp.dot(slot_rows, gate_matrix, preferred_element_type=jnp.float32)
    up_pre = jnp.dot(slot_rows, up_matrix, preferred_element_type=jnp.float32)
    sigmoid_gate = 1.0 / (1.0 + jnp.exp(-gate_pre))
    activated = gate_pre * sigmoid_gate
    hidden = (activated * up_pre).astype(jnp.bfloat16)
    grad_out = (weights[:, None] * slot_grads.astype(jnp.float32)).astype(jnp.bfloat16)
    grad_hidden = jnp.dot(grad_out, down_matrix.T, preferred_element_type=jnp.float32)
    grad_gate_pre = (grad_hidden * up_pre * (sigmoid_gate * (1.0 + gate_pre * (1.0 - sigmoid_gate)))).astype(jnp.bfloat16)
    grad_up_pre = (grad_hidden * activated).astype(jnp.bfloat16)
    slot_grad = jnp.dot(grad_gate_pre, gate_matrix.T, preferred_element_type=jnp.float32) + jnp.dot(grad_up_pre, up_matrix.T, preferred_element_type=jnp.float32)
    return grad_gate_pre, grad_up_pre, hidden, grad_out, slot_grad


def group_partials(slot_list, slot_rows, grad_gate_pre, grad_up_pre, hidden, grad_out):
    member = (slot_list // GROUP)[None, :] == jnp.arange(N_DP, dtype=jnp.int32)[:, None]
    picked, present = slot_ranks(member, ROWS)

    def gather_slots(values):
        return jnp.where(present[..., None], values[picked], jnp.zeros((), values.dtype))

    group_items = tuple(gather_slots(values) for values in (slot_rows, grad_gate_pre, grad_up_pre, hidden, grad_out))

    def group_step(running_sums, group_item):
        rows_here, gate_here, up_here, hidden_here, out_here = group_item
        sum_gate = running_sums[0] + rounded(jnp.dot(rows_here.T, gate_here, preferred_element_type=jnp.float32))
        sum_up = running_sums[1] + rounded(jnp.dot(rows_here.T, up_here, preferred_element_type=jnp.float32))
        sum_down = running_sums[2] + rounded(jnp.dot(hidden_here.T, out_here, preferred_element_type=jnp.float32))
        return (sum_gate, sum_up, sum_down), None

    start = (jnp.zeros((D, H), jnp.float32), jnp.zeros((D, H), jnp.float32), jnp.zeros((H, D), jnp.float32))
    sums, _ = lax.scan(group_step, start, group_items)
    return sums


def reference(tokens, out_grad, chosen, slot_weight, w_gate, w_up, w_down):
    dense_grad = jnp.zeros((TOKENS, D), jnp.float32)
    all_gate = []
    all_up = []
    all_down = []
    grad_scale = 1.0 / N_DP
    for expert in range(EXPERTS):
        slot_list = chosen[expert]
        slot_rows = tokens[slot_list]
        slot_grads = out_grad[slot_list]
        grad_gate_pre, grad_up_pre, hidden, grad_out, slot_grad = expert_pass(slot_rows, slot_grads, slot_weight[expert], w_gate[expert], w_up[expert], w_down[expert])
        sum_gate, sum_up, sum_down = group_partials(slot_list, slot_rows, grad_gate_pre, grad_up_pre, hidden, grad_out)
        all_gate.append((sum_gate * grad_scale).astype(jnp.bfloat16))
        all_up.append((sum_up * grad_scale).astype(jnp.bfloat16))
        all_down.append((sum_down * grad_scale).astype(jnp.bfloat16))
        dense_grad = dense_grad.at[slot_list].add(slot_grad)
    return (dense_grad.astype(jnp.bfloat16), jnp.stack(all_gate), jnp.stack(all_up), jnp.stack(all_down))
```

```python
import functools

import jax
import jax.numpy as jnp
from jax import lax
from jax.experimental import pallas as pl
from jax.experimental.pallas import tpu as pltpu
from jax.sharding import PartitionSpec as P

MESH = pl.DeviceIdType.MESH
BF = jnp.bfloat16
F32 = jnp.float32
MOST = 16
SLOTS = 64
QUARTER = 352
QPAD = 384
NN = (((1,), (0,)), ((), ()))
NT = (((1,), (1,)), ((), ()))
TN = (((0,), (0,)), ((), ()))


def dot(lhs, rhs, dims):
    return lax.dot_general(lhs, rhs, dims, preferred_element_type=F32)


def indicator(cond):
    return jnp.where(cond, 1.0, 0.0).astype(BF)


def route_kernel(chosen, slot_weight, tokens, out_grad, rows_out, grads_out, pick_out, weight_out,
                 tok_buf, grad_buf, sems):
    loads = [
        pltpu.make_async_copy(tokens, tok_buf, sems.at[0]),
        pltpu.make_async_copy(out_grad, grad_buf, sems.at[1]),
    ]
    for load in loads:
        load.start()
    dp = lax.axis_index("dp")
    me = lax.axis_index("expert")
    slots = chosen.shape[1]
    row = lax.broadcasted_iota(jnp.int32, (16, slots), 0)
    low_iota = lax.broadcasted_iota(jnp.int32, (128, slots), 0)
    counts = jnp.zeros((16, 128), F32)
    for n in range(4):
        entries = chosen[pl.ds((me + n) % 4, 1), :]
        high = (entries >> 7) - (dp * 4 + me) * 4
        high = jnp.where((high >= 0) & (high < 4), high + 4 * n, -1)
        counts = counts + dot(indicator(row == high), indicator(low_iota == (entries & 127)), NT)
    entries = chosen[pl.ds(me, 1), :]
    high = (entries >> 7) - dp * 16
    wanted = 4 * ((me + 4 - (row >> 2)) & 3) + (row & 3)
    hit = wanted == high
    low = indicator(low_iota == (entries & 127))
    group_counts = dot(indicator(hit), low, NT)
    value = slot_weight[...]
    part_a = value.astype(BF).astype(F32)
    part_b = (value - part_a).astype(BF).astype(F32)
    part_c = value - part_a - part_b
    weight_map = jnp.zeros((16, 128), F32)
    for part in (part_a, part_b, part_c):
        weight_map = weight_map + dot(jnp.where(hit, part, 0.0).astype(BF), low, NT)

    both = jnp.concatenate([counts, group_counts], axis=0)
    upper = indicator(
        lax.broadcasted_iota(jnp.int32, (128, 128), 0) <= lax.broadcasted_iota(jnp.int32, (128, 128), 1)
    )
    running = dot(both.astype(BF), upper, NN)
    totals = dot(both.astype(BF), jnp.ones((128, 128), BF), NN)
    left = lax.broadcasted_iota(jnp.int32, (32, 32), 0)
    right = lax.broadcasted_iota(jnp.int32, (32, 32), 1)
    before = indicator(((left >> 2) == (right >> 2)) & (right < left))
    rank = running + dot(before, totals.astype(BF), NN) - 1.0
    rank = jnp.where(both > 0.5, rank, -1.0)
    place = lax.broadcasted_iota(jnp.int32, (MOST, 512), 0).astype(F32)

    def line(values, first):
        return jnp.concatenate([values[first + h : first + h + 1, :] for h in range(4)], axis=1)

    for n in range(4):
        pick_out[16 * n : 16 * n + 16, :] = indicator(place == line(rank, 4 * n))
        chosen_here = jnp.where(place == line(rank, 16 + 4 * n), line(weight_map, 4 * n), 0.0)
        weight_out[16 * n : 16 * n + 16, :] = jnp.broadcast_to(
            jnp.sum(chosen_here, axis=1, keepdims=True), (MOST, 128)
        )
    loads[0].wait()
    rows_out[...] = dot(pick_out[...], tok_buf[...], NN).astype(BF)
    loads[1].wait()
    grads_out[...] = dot(pick_out[...], grad_buf[...], NN).astype(BF)


def route(chosen, slot_weight, tokens, out_grad):
    width = tokens.shape[1]
    vmem = pl.BlockSpec(memory_space=pltpu.VMEM)
    return pl.pallas_call(
        route_kernel,
        out_shape=(
            jax.ShapeDtypeStruct((SLOTS, width), BF),
            jax.ShapeDtypeStruct((SLOTS, width), BF),
            jax.ShapeDtypeStruct((SLOTS, tokens.shape[0]), BF),
            jax.ShapeDtypeStruct((SLOTS, 128), F32),
        ),
        in_specs=[vmem, vmem, pl.BlockSpec(memory_space=pl.ANY), pl.BlockSpec(memory_space=pl.ANY)],
        out_specs=(vmem,) * 4,
        scratch_shapes=[
            pltpu.VMEM(tokens.shape, BF),
            pltpu.VMEM(out_grad.shape, BF),
            pltpu.SemaphoreType.DMA((2,)),
        ],
        compiler_params=pltpu.CompilerParams(vmem_limit_bytes=32 * 2**20),
    )(chosen, slot_weight, tokens, out_grad)


def main_kernel(rows_in, grads_in, weight_in, w_gate, w_up, w_down, back_out, final_gu_out, final_d_out,
                wg, wu, wd, rows, raw, gout, rx, rg, rh, hq, ggp, gup, slot_send, back,
                part_gu, part_d, got_gu, got_d, fin_gu, fin_d, fg, fd,
                w_sem, disp_s, disp_r, early_s, early_r, late_s, late_r, ret_s, ret_r,
                sum_s, sum_r, gu_s, gu_r, d_s, d_r):
    dp = lax.axis_index("dp")
    me = lax.axis_index("expert")
    yl = dp % 2
    core = me % 2
    along_x = (dp // 2) % 4
    along_z = dp // 8
    a = along_x + core * (along_z - along_x)
    b = along_z + core * (along_x - along_z)

    def dp_of(a_at, b_at, y_at):
        return a_at * (2 + 6 * core) + b_at * (8 - 6 * core) + y_at

    def remote(src, dst, send_sem, recv_sem, target):
        return pltpu.make_async_remote_copy(
            src_ref=src, dst_ref=dst, send_sem=send_sem, recv_sem=recv_sem,
            device_id=target, device_id_type=MESH,
        )

    weights = []
    for n, (src, dst) in enumerate(((w_gate, wg), (w_up, wu), (w_down, wd))):
        half = dst.shape[0] // 2
        for h in range(2):
            part = pl.ds(h * half, half)
            weights.append(pltpu.make_async_copy(src.at[0, part], dst.at[part], w_sem.at[2 * n + h]))
    for copy in weights:
        copy.start()

    barrier = pltpu.get_barrier_semaphore()

    def greet(target):
        pl.semaphore_signal(barrier, inc=1, device_id=target, device_id_type=MESH)

    for n in range(1, 4):
        greet((dp, (me + n) % 4))
        greet((dp_of((a + n) % 4, b, yl), me))
        greet((dp_of((a + n) % 4, b, 1 - yl), me))
        greet((dp_of(a, (b + n) % 4, yl), me))
    greet((dp_of(a, b, 1 - yl), me))

    gu_sources = [dp_of(j, (dp % 16) // 4, dp // 16) for j in range(4)]
    d_sources = [dp_of(dp // 8, n % 4, n // 4) for n in range(8)]
    for source in gu_sources + d_sources:
        greet((source, me))
    pl.semaphore_wait(barrier, 25)

    block = lambda n: pl.ds(MOST * n, MOST)
    dispatch = [[], []]
    for which, (src, dst) in enumerate(((rows_in, rows), (grads_in, raw))):
        for n in (2, 1, 3):
            copy = remote(
                src.at[block(n)], dst.at[block(n)], disp_s.at[which, n], disp_r.at[which, n],
                (dp, (me + n) % 4),
            )
            copy.start()
            dispatch[which].append(copy)
    rows[0:MOST, :] = rows_in[0:MOST, :]
    raw[0:MOST, :] = grads_in[0:MOST, :]

    width = rows.shape[1]
    half = width // 2
    mine = pl.ds(pl.multiple_of(yl * half, half), half)
    other = pl.ds(pl.multiple_of((1 - yl) * half, half), half)
    slot = lambda y, d: pl.ds(SLOTS * (4 * y + d), SLOTS)

    def early_sends(which, src, dst):
        copies = [remote(
            src.at[:, other], dst.at[slot(1, 0)], early_s.at[which, 0], early_r.at[which, 0],
            (dp_of(a, b, 1 - yl), me),
        )]
        for n in (2, 1, 3):
            copies.append(remote(
                src.at[:, mine], dst.at[slot(0, n)], early_s.at[which, n], early_r.at[which, n],
                (dp_of((a + n) % 4, b, yl), me),
            ))
        for copy in copies:
            copy.start()
        dst[0:SLOTS, :] = src[:, mine]
        return copies

    def forward_sends(which, dst):
        copies = []
        for n in (2, 1, 3):
            copy = remote(
                dst.at[slot(1, 0)], dst.at[slot(1, n)], early_s.at[which, 3 + n], early_r.at[which, 3 + n],
                (dp_of((a + n) % 4, b, yl), me),
            )
            copy.start()
            copies.append(copy)
        return copies

    for copy in dispatch[0]:
        copy.wait_recv()
    early = early_sends(0, rows, rx)
    for copy in weights[0:4]:
        copy.wait()
    gate_pre = dot(rows[...], wg[...], NN)
    up_pre = dot(rows[...], wu[...], NN)
    for copy in dispatch[1]:
        copy.wait_recv()
    gout[...] = (weight_in[:, 0:1] * raw[...].astype(F32)).astype(BF)
    early_g = early_sends(1, gout, rg)
    sig = 1.0 / (1.0 + jnp.exp(-gate_pre))
    activated = gate_pre * sig
    hidden = (activated * up_pre).astype(BF)
    early[0].wait_recv()
    forwards = forward_sends(0, rx)
    for copy in weights[4:6]:
        copy.wait()
    grad_hidden = dot(gout[...], wd[...], NT)
    ggp[...] = (grad_hidden * up_pre * (sig * (1.0 + gate_pre * (1.0 - sig)))).astype(BF)
    gup[...] = (grad_hidden * activated).astype(BF)
    blank = jnp.zeros((SLOTS, QPAD - QUARTER), BF)
    for n, value in enumerate((ggp[...], gup[...], hidden)):
        for j in range(4):
            hq[j, :, QPAD * n : QPAD * (n + 1)] = jnp.concatenate(
                [value[:, QUARTER * j : QUARTER * (j + 1)], blank], axis=1
            )

    late = []
    for y, n in ((1, 2), (1, 1), (1, 3), (1, 0), (0, 2), (0, 1), (0, 3)):
        at = (a + n) % 4
        copy = remote(
            hq.at[at], rh.at[slot(y, n)], late_s.at[4 * y + n], late_r.at[4 * y + n],
            (dp_of(at, b, yl + y * (1 - 2 * yl)), me),
        )
        copy.start()
        late.append(copy)
    rh[0:SLOTS, :] = hq[a]
    early_g[0].wait_recv()
    forwards += forward_sends(1, rg)

    slot_grad = dot(ggp[...], wg[...], NT) + dot(gup[...], wu[...], NT)
    slot_send[...] = slot_grad.astype(BF)
    returns = []
    for n in (2, 1, 3):
        copy = remote(
            slot_send.at[block(n)], back.at[block(n)], ret_s.at[n], ret_r.at[n],
            (dp, (me + 4 - n) % 4),
        )
        copy.start()
        returns.append(copy)
    back[0:MOST, :] = slot_send[0:MOST, :]

    for copy in early[1:] + early_g[1:] + forwards + late:
        copy.wait_recv()

    chunk = half // 4
    sums = []
    for n in (2, 1, 3, 0):
        at = (b + n) % 4
        columns = pl.ds(pl.multiple_of(at * chunk, chunk), chunk)
        part_gu[n] = dot(rx[:, columns], rh[:, 0 : 2 * QPAD], TN).astype(BF)
        part_d[n] = dot(rh[:, 2 * QPAD : 3 * QPAD], rg[:, columns], TN).astype(BF)
        if n:
            target = (dp_of(a, at, yl), me)
            for which, (src, dst) in enumerate(((part_gu, got_gu), (part_d, got_d))):
                copy = remote(
                    src.at[n], dst.at[n], sum_s.at[which, n], sum_r.at[which, n], target
                )
                copy.start()
                sums.append(copy)

    for copy in returns:
        copy.wait_recv()
    back_out[...] = back[...]

    for copy in sums:
        copy.wait_recv()
    scale = 1.0 / 32
    total = part_gu[0].astype(F32)
    for n in range(1, 4):
        total = total + got_gu[n].astype(F32)
    fin_gu[...] = (total * scale).astype(BF)
    total = part_d[0].astype(F32)
    for n in range(1, 4):
        total = total + got_d[n].astype(F32)
    total = total * scale
    spare = jnp.zeros((4, chunk), F32)
    for m in range(8):
        fin_d[m] = jnp.concatenate([total[44 * m : 44 * m + 44, :], spare], axis=0).astype(BF)

    def place(src, dst, send_sem, recv_sem, owner):
        copy = remote(src, dst, send_sem, recv_sem, (owner, me))

        @pl.when(owner != dp)
        def _():
            copy.start()

        @pl.when(owner == dp)
        def _():
            pltpu.make_async_copy(src, dst, recv_sem).start()

        return owner, copy

    placed = []
    for m in range(4):
        placed.append(place(
            fin_gu.at[pl.ds(64 * m, 64)], fg.at[a], gu_s.at[m], gu_r.at[a], 16 * yl + 4 * b + m
        ))
    for m in range(8):
        placed.append(place(
            fin_d.at[m], fd.at[4 * yl + b], d_s.at[m], d_r.at[4 * yl + b], 8 * a + m
        ))
    for j in range(4):
        pltpu.make_async_copy(fg.at[j], fg.at[j], gu_r.at[j]).wait()
    for n in range(8):
        pltpu.make_async_copy(fd.at[n], fd.at[n], d_r.at[n]).wait()
    final_gu_out[...] = fg[...]
    final_d_out[...] = fd[...]

    for copy in dispatch[0] + dispatch[1] + early + early_g + forwards + late + returns + sums:
        copy.wait_send()
    for owner, copy in placed:
        @pl.when(owner != dp)
        def _():
            copy.wait_send()


def main_pass(rows, grads, weights, w_gate, w_up, w_down):
    width = rows.shape[1]
    hid = w_gate.shape[2]
    half = width // 2
    chunk = half // 4
    vmem = pl.BlockSpec(memory_space=pltpu.VMEM)
    hbm = pl.BlockSpec(memory_space=pl.ANY)
    dma = pltpu.SemaphoreType.DMA
    return pl.pallas_call(
        main_kernel,
        out_shape=(
            jax.ShapeDtypeStruct((SLOTS, width), BF),
            jax.ShapeDtypeStruct((4, 64, 2 * QPAD), BF),
            jax.ShapeDtypeStruct((8, 48, chunk), BF),
        ),
        in_specs=[vmem, vmem, vmem, hbm, hbm, hbm],
        out_specs=(vmem,) * 3,
        scratch_shapes=[
            pltpu.VMEM((width, hid), BF),
            pltpu.VMEM((width, hid), BF),
            pltpu.VMEM((hid, width), BF),
            pltpu.VMEM((SLOTS, width), BF),
            pltpu.VMEM((SLOTS, width), BF),
            pltpu.VMEM((SLOTS, width), BF),
            pltpu.VMEM((8 * SLOTS, half), BF),
            pltpu.VMEM((8 * SLOTS, half), BF),
            pltpu.VMEM((8 * SLOTS, 3 * QPAD), BF),
            pltpu.VMEM((4, SLOTS, 3 * QPAD), BF),
            pltpu.VMEM((SLOTS, hid), BF),
            pltpu.VMEM((SLOTS, hid), BF),
            pltpu.VMEM((SLOTS, width), BF),
            pltpu.VMEM((SLOTS, width), BF),
            pltpu.VMEM((4, chunk, 2 * QPAD), BF),
            pltpu.VMEM((4, QPAD, chunk), BF),
            pltpu.VMEM((4, chunk, 2 * QPAD), BF),
            pltpu.VMEM((4, QPAD, chunk), BF),
            pltpu.VMEM((chunk, 2 * QPAD), BF),
            pltpu.VMEM((8, 48, chunk), BF),
            pltpu.VMEM((4, 64, 2 * QPAD), BF),
            pltpu.VMEM((8, 48, chunk), BF),
            dma((6,)),
            dma((2, 4)), dma((2, 4)),
            dma((2, 7)), dma((2, 7)),
            dma((8,)), dma((8,)),
            dma((4,)), dma((4,)),
            dma((2, 4)), dma((2, 4)),
            dma((4,)), dma((4,)),
            dma((8,)), dma((8,)),
        ],
        compiler_params=pltpu.CompilerParams(
            collective_id=0, has_side_effects=True, vmem_limit_bytes=56 * 2**20
        ),
    )(rows, grads, weights, w_gate, w_up, w_down)


def finish_kernel(pick, back, final_gu, final_d, token_grad, grad_gate, grad_up, grad_down):
    for n in range(4):
        part = pl.ds(128 * n, 128)
        token_grad[part, :] = dot(pick[:, part], back[...], TN).astype(BF)
    for j in range(4):
        grad_gate[0, :, QUARTER * j : QUARTER * (j + 1)] = final_gu[j, :, 0:QUARTER]
        grad_up[0, :, QUARTER * j : QUARTER * (j + 1)] = final_gu[j, :, QPAD : QPAD + QUARTER]
    for n in range(8):
        grad_down[0, :, 256 * n : 256 * (n + 1)] = final_d[n, 0:44, :]


def finish(pick, back, final_gu, final_d, hid):
    width = back.shape[1]
    vmem = pl.BlockSpec(memory_space=pltpu.VMEM)
    return pl.pallas_call(
        finish_kernel,
        out_shape=(
            jax.ShapeDtypeStruct((pick.shape[1], width), BF),
            jax.ShapeDtypeStruct((1, width // 32, hid), BF),
            jax.ShapeDtypeStruct((1, width // 32, hid), BF),
            jax.ShapeDtypeStruct((1, hid // 32, width), BF),
        ),
        in_specs=[vmem] * 4,
        out_specs=(vmem,) * 4,
        compiler_params=pltpu.CompilerParams(vmem_limit_bytes=32 * 2**20),
    )(pick, back, final_gu, final_d)


def local(tokens, out_grad, chosen, slot_weight, w_gate, w_up, w_down):
    rows, grads, pick, weights = route(chosen, slot_weight, tokens, out_grad)
    back, final_gu, final_d = main_pass(rows, grads, weights, w_gate, w_up, w_down)
    return finish(pick, back, final_gu, final_d, w_gate.shape[2])


def solution(mesh):
    return jax.shard_map(
        local,
        mesh=mesh,
        in_specs=(
            P(("dp", "expert"), None),
            P(("dp", "expert"), None),
            P(),
            P("expert", None),
            P("expert", None, None),
            P("expert", None, None),
            P("expert", None, None),
        ),
        out_specs=(
            P(("dp", "expert"), None),
            P("expert", "dp", None),
            P("expert", "dp", None),
            P("expert", "dp", None),
        ),
        check_vma=False,
    )
```

```python
import jax
import jax.numpy as jnp
from jax import lax
from jax.experimental import pallas as pl
from jax.experimental.pallas import tpu as pltpu
from jax.sharding import PartitionSpec as P

MESH = pl.DeviceIdType.MESH
BF = jnp.bfloat16
F32 = jnp.float32
MOST = 16
SLOTS = 64
QUARTER = 352
QPAD = 384
NN = (((1,), (0,)), ((), ()))
NT = (((1,), (1,)), ((), ()))
TN = (((0,), (0,)), ((), ()))


def dot(lhs, rhs, dims):
    return lax.dot_general(lhs, rhs, dims, preferred_element_type=F32)


def indicator(cond):
    return jnp.where(cond, 1.0, 0.0).astype(BF)


def route(me, dp, chosen, slot_weight, pick, weight):
    slots = chosen.shape[1]
    row = lax.broadcasted_iota(jnp.int32, (16, slots), 0)
    low_iota = lax.broadcasted_iota(jnp.int32, (128, slots), 0)
    lists = chosen[...]
    counts = jnp.zeros((16, 128), F32)
    group_counts = jnp.zeros((16, 128), F32)
    weight_map = jnp.zeros((16, 128), F32)
    value = slot_weight[...]
    part_a = value.astype(BF).astype(F32)
    part_b = (value - part_a).astype(BF).astype(F32)
    part_c = value - part_a - part_b
    for f in range(4):
        entries = lists[f : f + 1, :]
        low = indicator(low_iota == (entries & 127))
        tile = entries >> 7
        high = tile - (dp * 4 + me) * 4
        n = (f + 4 - me) % 4
        high = jnp.where((high >= 0) & (high < 4), high + 4 * n, -1)
        counts = counts + dot(indicator(row == high), low, NT)
        if f == 0:
            mine, mine_low = tile, low
        else:
            is_mine = me == f
            mine = jnp.where(is_mine, tile, mine)
            mine_low = jnp.where(is_mine, low, mine_low)
    wanted = 4 * ((me + 4 - (row >> 2)) & 3) + (row & 3)
    hit = wanted == mine - dp * 16
    stacked = jnp.concatenate(
        [jnp.where(hit, part, 0.0).astype(BF) for part in (jnp.ones_like(value), part_a, part_b, part_c)],
        axis=0,
    )
    found = dot(stacked, mine_low, NT)
    group_counts = found[0:16]
    weight_map = found[16:32] + found[32:48] + found[48:64]

    both = jnp.concatenate([counts, group_counts], axis=0)
    upper = indicator(
        lax.broadcasted_iota(jnp.int32, (128, 128), 0) <= lax.broadcasted_iota(jnp.int32, (128, 128), 1)
    )
    running = dot(both.astype(BF), upper, NN)
    totals = dot(both.astype(BF), jnp.ones((128, 128), BF), NN)
    left = lax.broadcasted_iota(jnp.int32, (32, 32), 0)
    right = lax.broadcasted_iota(jnp.int32, (32, 32), 1)
    before = indicator(((left >> 2) == (right >> 2)) & (right < left))
    rank = running + dot(before, totals.astype(BF), NN) - 1.0
    rank = jnp.where(both > 0.5, rank, -1.0)
    place = lax.broadcasted_iota(jnp.int32, (MOST, 512), 0).astype(F32)

    def line(values, first):
        return jnp.concatenate([values[first + h : first + h + 1, :] for h in range(4)], axis=1)

    for n in range(4):
        pick[16 * n : 16 * n + 16, :] = indicator(place == line(rank, 4 * n))
        chosen_here = jnp.where(place == line(rank, 16 + 4 * n), line(weight_map, 4 * n), 0.0)
        weight[16 * n : 16 * n + 16, :] = jnp.broadcast_to(
            jnp.sum(chosen_here, axis=1, keepdims=True), (MOST, 128)
        )


def main_kernel(chosen, slot_weight, tokens, out_grad, w_gate, w_up, w_down,
                pick, back, fin_g, fin_u, fin_d,
                tok_buf, grad_buf, weight, rows_in, grads_in, wg, wu, wd, rows, raw, gout, xh, gh, rx, rg,
                rh, hq, ggp, gup, slot_send, back_buf, part_d, got_d, part_gu, got_gu, out_d, out_gu,
                land_d, land_gu,
                load_sem, w_sem, disp_s, disp_r, early_s, early_r, late_s, late_r, cross_s, cross_r,
                ret_s, ret_r, sum_s, sum_r, put_s, put_r):
    dp = lax.axis_index("dp")
    me = lax.axis_index("expert")
    yl = dp % 2
    core = me % 2
    along_x = (dp // 2) % 4
    along_z = dp // 8
    a = along_x + core * (along_z - along_x)
    b = along_z + core * (along_x - along_z)

    def at_dp(a_at, b_at, y_at):
        return a_at * (2 + 6 * core) + b_at * (8 - 6 * core) + y_at

    ring_a = [(at_dp((a + n) % 4, b, yl), me) for n in range(4)]
    ring_b = [(at_dp(a, (b + n) % 4, yl), me) for n in range(4)]
    across = (at_dp(a, b, 1 - yl), me)
    started = []

    def send(src, dst, send_sem, recv_sem, target):
        copy = pltpu.make_async_remote_copy(
            src_ref=src, dst_ref=dst, send_sem=send_sem, recv_sem=recv_sem,
            device_id=target, device_id_type=MESH,
        )
        copy.start()
        started.append(copy)
        return copy

    loads = [
        pltpu.make_async_copy(tokens, tok_buf, load_sem.at[0]),
        pltpu.make_async_copy(out_grad, grad_buf, load_sem.at[1]),
    ]
    weights = []
    for n, (src, dst) in enumerate(((w_gate, wg), (w_up, wu), (w_down, wd))):
        half = dst.shape[0] // 2
        for h in range(2):
            part = pl.ds(h * half, half)
            weights.append(pltpu.make_async_copy(src.at[0, part], dst.at[part], w_sem.at[2 * n + h]))
    for copy in loads + weights:
        copy.start()

    barrier = pltpu.get_barrier_semaphore()
    friends = [(dp, (me + n) % 4) for n in range(1, 4)] + ring_a[1:] + ring_b[1:] + [across]
    for friend in friends:
        pl.semaphore_signal(barrier, inc=1, device_id=friend, device_id_type=MESH)

    route(me, dp, chosen, slot_weight, pick, weight)
    loads[0].wait()
    rows_in[...] = dot(pick[...], tok_buf[...], NN).astype(BF)
    pl.semaphore_wait(barrier, len(friends))

    block = lambda n: pl.ds(MOST * n, MOST)

    def dispatch(which, src, dst):
        copies = [
            send(src.at[block(n)], dst.at[block(n)], disp_s.at[which, n], disp_r.at[which, n],
                 (dp, (me + n) % 4))
            for n in (2, 3, 1)
        ]
        dst[0:MOST, :] = src[0:MOST, :]
        return copies

    row_copies = dispatch(0, rows_in, rows)
    loads[1].wait()
    grads_in[...] = dot(pick[...], grad_buf[...], NN).astype(BF)
    grad_copies = dispatch(1, grads_in, raw)

    half = rows.shape[1] // 2
    slot = lambda y, d: pl.ds(SLOTS * (4 * y + d), SLOTS)

    def early_sends(which, src, dst):
        copies = [send(src.at[1 - yl], dst.at[slot(1, 0)], early_s.at[which, 0], early_r.at[which, 0], across)]
        for n in (2, 1, 3):
            copies.append(send(
                src.at[yl], dst.at[slot(0, n)], early_s.at[which, n], early_r.at[which, n], ring_a[n]
            ))
        dst[0:SLOTS, :] = src[yl]
        return copies

    def early_forward(which, dst):
        return [
            send(dst.at[slot(1, 0)], dst.at[slot(1, n)], early_s.at[which, 3 + n],
                 early_r.at[which, 3 + n], ring_a[n])
            for n in (2, 1, 3)
        ]

    for copy in row_copies:
        copy.wait_recv()
    for which in range(2):
        @pl.when(core == which)
        def _():
            for y in range(2):
                order = [u if which == 0 else 4 * (u % 4) + u // 4 for u in range(16)]
                xh[y] = jnp.concatenate(
                    [rows[:, 128 * u + 64 * y : 128 * u + 64 * y + 64] for u in order], axis=1
                )
    early_x = early_sends(0, xh, rx)

    for copy in weights[0:4]:
        copy.wait()
    gate_pre = dot(rows[...], wg[...], NN)
    up_pre = dot(rows[...], wu[...], NN)
    sig = 1.0 / (1.0 + jnp.exp(-gate_pre))
    activated = gate_pre * sig
    ggp[...] = (activated * up_pre).astype(BF)
    gap = jnp.zeros((SLOTS, 4), BF)
    for which in range(2):
        @pl.when(core == which)
        def _():
            for j in range(4):
                pieces = []
                for v in range(8):
                    owner = (v // 2) * 8 + 2 * j + v % 2 if which == 0 else 8 * j + v
                    pieces += [ggp[:, 44 * owner : 44 * owner + 44], gap]
                hq[0, j] = jnp.concatenate(pieces, axis=1)

    def late_sends(part):
        copies = [None] + [
            send(hq.at[part, (a + n) % 4], rh.at[part, slot(0, n)], late_s.at[part, n], late_r.at[part, n],
                 ring_a[n])
            for n in (1, 2, 3)
        ]
        rh[part, 0:SLOTS, :] = hq[part, a]
        crossed = [send(hq.at[part, a], rh.at[part, slot(1, 0)], cross_s.at[part, 0], cross_r.at[part, 0], across)]
        return copies, crossed

    def late_cross(part, copies):
        crossed = []
        for n in (1, 3, 2):
            copies[n].wait_recv()
            crossed.append(send(
                rh.at[part, slot(0, n)], rh.at[part, slot(1, n)], cross_s.at[part, n], cross_r.at[part, n], across
            ))
        return crossed

    late = [None] * 3
    crossed = [None] * 3
    late[0], crossed[0] = late_sends(0)

    for copy in grad_copies:
        copy.wait_recv()
    gout[...] = (weight[:, 0:1] * raw[...].astype(F32)).astype(BF)
    for y in range(2):
        gh[y] = gout[:, half * y : half * (y + 1)]
    early_g = early_sends(1, gh, rg)
    early_x[0].wait_recv()
    early_x += early_forward(0, rx)

    for copy in weights[4:6]:
        copy.wait()
    grad_hidden = dot(gout[...], wd[...], NT)
    gup[...] = (grad_hidden * activated).astype(BF)
    ggp[...] = (grad_hidden * up_pre * (sig * (1.0 + gate_pre * (1.0 - sig)))).astype(BF)
    blank = jnp.zeros((SLOTS, QPAD - QUARTER), BF)
    for part, value in ((1, gup), (2, ggp)):
        for j in range(4):
            hq[part, j] = jnp.concatenate([value[:, QUARTER * j : QUARTER * (j + 1)], blank], axis=1)
        late[part], crossed[part] = late_sends(part)
    crossed[0] += late_cross(0, late[0])
    early_g[0].wait_recv()
    early_g += early_forward(1, rg)
    crossed[1] += late_cross(1, late[1])
    crossed[2] += late_cross(2, late[2])

    slot_grad = dot(ggp[...], wg[...], NT) + dot(gup[...], wu[...], NT)
    slot_send[...] = slot_grad.astype(BF)
    returns = [
        send(slot_send.at[block(n)], back_buf.at[block(n)], ret_s.at[n], ret_r.at[n], (dp, (me + 4 - n) % 4))
        for n in (2, 1, 3)
    ]
    back_buf[0:MOST, :] = slot_send[0:MOST, :]

    chunk = half // 4
    sums = [[], [], []]
    for copy in early_g[1:] + crossed[0]:
        copy.wait_recv()
    part_d[...] = dot(rh[0], rg[...], TN).astype(BF)
    rows_d = QPAD // 4
    for n in (2, 1, 3):
        sums[0].append(send(
            part_d.at[pl.ds(pl.multiple_of((b + n) % 4 * rows_d, rows_d), rows_d)], got_d.at[n],
            sum_s.at[0, n], sum_r.at[0, n], ring_b[n],
        ))
    for copy in early_x[1:]:
        copy.wait_recv()
    for part in (1, 2):
        for copy in crossed[part]:
            copy.wait_recv()
        for n in (2, 1, 3, 0):
            columns = pl.ds(pl.multiple_of((b + n) % 4 * chunk, chunk), chunk)
            part_gu[part - 1, n] = dot(rx[:, columns], rh[part], TN).astype(BF)
            if n:
                sums[part].append(send(
                    part_gu.at[part - 1, n], got_gu.at[part - 1, n],
                    sum_s.at[part, n], sum_r.at[part, n], ring_b[n],
                ))

    scale = 1.0 / 32
    for copy in sums[0]:
        copy.wait_recv()
    total = part_d[pl.ds(pl.multiple_of(b * rows_d, rows_d), rows_d), :].astype(F32)
    for n in range(1, 4):
        total = total + got_d[n].astype(F32)
    out_d[...] = (total * scale).astype(BF).reshape(out_d.shape)
    put_d = send(out_d.at[1 - yl], land_d.at[yl], put_s.at[0, 0], put_r.at[0, 0], across)
    land_d[yl] = out_d[yl]
    puts = []
    for part in (1, 2):
        for copy in sums[part]:
            copy.wait_recv()
        total = part_gu[part - 1, 0].astype(F32)
        for n in range(1, 4):
            total = total + got_gu[part - 1, n].astype(F32)
        out_gu[part - 1] = (total * scale).astype(BF).reshape(out_gu.shape[1:])
        for n in (2, 1, 3):
            puts.append(send(
                out_gu.at[part - 1, (a + n) % 4], land_gu.at[part - 1, a], put_s.at[part, n], put_r.at[part, n],
                ring_a[n],
            ))
        land_gu[part - 1, a] = out_gu[part - 1, a]

    for copy in returns:
        copy.wait_recv()
    back[...] = back_buf[...]
    pltpu.make_async_copy(land_d.at[1 - yl], land_d.at[1 - yl], put_r.at[0, 0]).wait()
    fin_d[...] = land_d[...]
    for part, dst in ((1, fin_u), (2, fin_g)):
        for n in (1, 2, 3):
            there = land_gu.at[part - 1, (a + 4 - n) % 4]
            pltpu.make_async_copy(there, there, put_r.at[part, n]).wait()
        dst[...] = land_gu[part - 1]
    for copy in started:
        copy.wait_send()


def main_pass(chosen, slot_weight, tokens, out_grad, w_gate, w_up, w_down):
    width = tokens.shape[1]
    hid = w_gate.shape[2]
    half = width // 2
    chunk = half // 4
    vmem = pl.BlockSpec(memory_space=pltpu.VMEM)
    hbm = pl.BlockSpec(memory_space=pl.ANY)
    dma = pltpu.SemaphoreType.DMA

    def buf(*shape):
        return pltpu.VMEM(shape, BF)

    return pl.pallas_call(
        main_kernel,
        out_shape=(
            jax.ShapeDtypeStruct((SLOTS, tokens.shape[0]), BF),
            jax.ShapeDtypeStruct((SLOTS, width), BF),
            jax.ShapeDtypeStruct((4, 64, QPAD), BF),
            jax.ShapeDtypeStruct((4, 64, QPAD), BF),
            jax.ShapeDtypeStruct((2, 48, half), BF),
        ),
        in_specs=[vmem, vmem, hbm, hbm, hbm, hbm, hbm],
        out_specs=(vmem,) * 5,
        scratch_shapes=[
            buf(*tokens.shape), buf(*tokens.shape),
            pltpu.VMEM((SLOTS, 128), F32),
            buf(SLOTS, width), buf(SLOTS, width),
            buf(width, hid), buf(width, hid), buf(hid, width),
            buf(SLOTS, width), buf(SLOTS, width), buf(SLOTS, width),
            buf(2, SLOTS, half), buf(2, SLOTS, half),
            buf(8 * SLOTS, half), buf(8 * SLOTS, half),
            buf(3, 8 * SLOTS, QPAD), buf(3, 4, SLOTS, QPAD),
            buf(SLOTS, hid), buf(SLOTS, hid),
            buf(SLOTS, width), buf(SLOTS, width),
            buf(QPAD, half), buf(4, QPAD // 4, half),
            buf(2, 4, chunk, QPAD), buf(2, 4, chunk, QPAD),
            buf(2, 48, half), buf(2, 4, 64, QPAD),
            buf(2, 48, half), buf(2, 4, 64, QPAD),
            dma((2,)), dma((6,)),
            dma((2, 4)), dma((2, 4)),
            dma((2, 7)), dma((2, 7)),
            dma((3, 4)), dma((3, 4)),
            dma((3, 4)), dma((3, 4)),
            dma((4,)), dma((4,)),
            dma((3, 4)), dma((3, 4)),
            dma((3, 4)), dma((3, 4)),
        ],
        compiler_params=pltpu.CompilerParams(
            collective_id=0, has_side_effects=True, vmem_limit_bytes=60 * 2**20
        ),
    )(chosen, slot_weight, tokens, out_grad, w_gate, w_up, w_down)


def finish_kernel(pick, back, fin_g, fin_u, fin_d, token_grad, grad_gate, grad_up, grad_down):
    for n in range(4):
        part = pl.ds(128 * n, 128)
        token_grad[part, :] = dot(pick[:, part], back[...], TN).astype(BF)
    for j in range(4):
        grad_gate[0, :, QUARTER * j : QUARTER * (j + 1)] = fin_g[j, :, 0:QUARTER]
        grad_up[0, :, QUARTER * j : QUARTER * (j + 1)] = fin_u[j, :, 0:QUARTER]
    half = fin_d.shape[2]
    for y in range(2):
        grad_down[0, :, half * y : half * (y + 1)] = fin_d[y, 0:44, :]


def finish(pick, back, fin_g, fin_u, fin_d, hid):
    width = back.shape[1]
    vmem = pl.BlockSpec(memory_space=pltpu.VMEM)
    return pl.pallas_call(
        finish_kernel,
        out_shape=(
            jax.ShapeDtypeStruct((pick.shape[1], width), BF),
            jax.ShapeDtypeStruct((1, width // 32, hid), BF),
            jax.ShapeDtypeStruct((1, width // 32, hid), BF),
            jax.ShapeDtypeStruct((1, hid // 32, width), BF),
        ),
        in_specs=[vmem] * 5,
        out_specs=(vmem,) * 4,
        compiler_params=pltpu.CompilerParams(vmem_limit_bytes=60 * 2**20),
    )(pick, back, fin_g, fin_u, fin_d)


def local(tokens, out_grad, chosen, slot_weight, w_gate, w_up, w_down):
    pick, back, fin_g, fin_u, fin_d = main_pass(
        chosen, slot_weight, tokens, out_grad, w_gate, w_up, w_down
    )
    return finish(pick, back, fin_g, fin_u, fin_d, w_gate.shape[2])


def solution(mesh):
    return jax.shard_map(
        local,
        mesh=mesh,
        in_specs=(
            P(("dp", "expert"), None),
            P(("dp", "expert"), None),
            P(),
            P("expert", None),
            P("expert", None, None),
            P("expert", None, None),
            P("expert", None, None),
        ),
        out_specs=(
            P(("dp", "expert"), None),
            P("expert", "dp", None),
            P("expert", "dp", None),
            P("expert", "dp", None),
        ),
        check_vma=False,
    )
```

```python
import jax
import jax.numpy as jnp
from jax import lax
from jax.experimental import pallas as pl
from jax.experimental.pallas import tpu as pltpu
from jax.sharding import PartitionSpec as P

MESH = pl.DeviceIdType.MESH
BF = jnp.bfloat16
F32 = jnp.float32
MOST = 16
SLOTS = 64
QUARTER = 352
QPAD = 384
NN = (((1,), (0,)), ((), ()))
NT = (((1,), (1,)), ((), ()))
TN = (((0,), (0,)), ((), ()))


def dot(lhs, rhs, dims):
    return lax.dot_general(lhs, rhs, dims, preferred_element_type=F32)


def indicator(cond):
    return jnp.where(cond, 1.0, 0.0).astype(BF)


def route(me, dp, near, chosen, slot_weight, pick, weight):
    slots = chosen.shape[1]
    row = lax.broadcasted_iota(jnp.int32, (16, slots), 0)
    low_iota = lax.broadcasted_iota(jnp.int32, (128, slots), 0)
    lists = chosen[...]
    counts = jnp.zeros((16, 128), F32)
    value = slot_weight[...]
    part_a = value.astype(BF).astype(F32)
    part_b = (value - part_a).astype(BF).astype(F32)
    part_c = value - part_a - part_b
    for f in range(4):
        entries = lists[f : f + 1, :]
        low = indicator(low_iota == (entries & 127))
        tile = entries >> 7
        high = tile - (dp * 4 + me) * 4
        n = (f + 4 - me) % 4
        high = jnp.where((high >= 0) & (high < 4), high + 4 * n, -1)
        counts = counts + dot(indicator(row == high), low, NT)
        if f == 0:
            mine, mine_low = tile, low
        else:
            is_mine = me == f
            mine = jnp.where(is_mine, tile, mine)
            mine_low = jnp.where(is_mine, low, mine_low)
    wanted = 4 * ((me + 4 - (row >> 2)) & 3) + (row & 3)
    stacked = []
    for part in (jnp.ones_like(value), part_a, part_b, part_c):
        for group in (dp, near):
            stacked.append(jnp.where(wanted == mine - group * 16, part, 0.0).astype(BF))
    found = dot(jnp.concatenate(stacked, axis=0), mine_low, NT)
    weight_map = found[32:64] + found[64:96] + found[96:128]

    both = jnp.concatenate([counts, found[0:32]], axis=0)
    upper = indicator(
        lax.broadcasted_iota(jnp.int32, (128, 128), 0) <= lax.broadcasted_iota(jnp.int32, (128, 128), 1)
    )
    running = dot(both.astype(BF), upper, NN)
    totals = dot(both.astype(BF), jnp.ones((128, 128), BF), NN)
    left = lax.broadcasted_iota(jnp.int32, (48, 48), 0)
    right = lax.broadcasted_iota(jnp.int32, (48, 48), 1)
    before = indicator(((left >> 2) == (right >> 2)) & (right < left))
    rank = running + dot(before, totals.astype(BF), NN) - 1.0
    rank = jnp.where(both > 0.5, rank, -1.0)
    place = lax.broadcasted_iota(jnp.int32, (MOST, 512), 0).astype(F32)

    def line(values, first):
        return jnp.concatenate([values[first + h : first + h + 1, :] for h in range(4)], axis=1)

    for n in range(4):
        pick[16 * n : 16 * n + 16, :] = indicator(place == line(rank, 4 * n))
    for n in range(8):
        chosen_here = jnp.where(place == line(rank, 16 + 4 * n), line(weight_map, 4 * n), 0.0)
        weight[16 * n : 16 * n + 16, :] = jnp.broadcast_to(
            jnp.sum(chosen_here, axis=1, keepdims=True), (MOST, 128)
        )


def main_kernel(chosen_in, slot_weight_in, tokens, out_grad, w_gate, w_up, w_down,
                token_grad, grad_gate, grad_up, grad_down,
                chosen, slot_weight, pick, tok_buf, grad_buf, weight, rows_in, grads_in, wg, wu, wd,
                rows, raw, gout, rx, rg, rh, rgu, hq, gq, ggp, gup, slot_send, back, part_d, got_d,
                part_gu, got_gu, out_d, out_gu, land_d, land_gu,
                load_sem, w_sem, disp_s, disp_r, early_s, early_r, late_s, late_r,
                ret_s, ret_r, sum_s, sum_r, put_s, put_r):
    dp = lax.axis_index("dp")
    me = lax.axis_index("expert")
    yl = dp % 2
    core = me % 2
    along_x = (dp // 2) % 4
    along_z = dp // 8
    a = along_x + core * (along_z - along_x)
    b = along_z + core * (along_x - along_z)

    def at_dp(a_at, b_at, y_at):
        return a_at * (2 + 6 * core) + b_at * (8 - 6 * core) + y_at

    ring_a = [(at_dp((a + n) % 4, b, yl), me) for n in range(4)]
    ring_b = [(at_dp(a, (b + n) % 4, yl), me) for n in range(4)]
    across = (at_dp(a, b, 1 - yl), me)
    started = []

    def send(src, dst, send_sem, recv_sem, target):
        copy = pltpu.make_async_remote_copy(
            src_ref=src, dst_ref=dst, send_sem=send_sem, recv_sem=recv_sem,
            device_id=target, device_id_type=MESH,
        )
        copy.start()
        started.append(copy)
        return copy

    barrier = pltpu.get_barrier_semaphore()
    near = dp + 1 - 2 * yl
    group = [(dp, (me + n) % 4) for n in range(4)]
    near_group = [(near, (me + n) % 4) for n in range(4)]
    friends = group[1:] + near_group + ring_a[1:] + ring_b[1:]
    for friend in friends:
        pl.semaphore_signal(barrier, inc=1, device_id=friend, device_id_type=MESH)

    loads = [
        pltpu.make_async_copy(src, dst, load_sem.at[n])
        for n, (src, dst) in enumerate(
            ((chosen_in, chosen), (slot_weight_in, slot_weight), (tokens, tok_buf), (out_grad, grad_buf))
        )
    ]
    weights = []
    for n, (src, dst) in enumerate(((w_gate, wg), (w_up, wu), (w_down, wd))):
        middle = dst.shape[0] // 2
        for h in range(2):
            part = pl.ds(h * middle, middle)
            weights.append(pltpu.make_async_copy(src.at[0, part], dst.at[part], w_sem.at[2 * n + h]))
    for copy in loads:
        copy.start()
    for copy in loads[0:2]:
        copy.wait()
    route(me, dp, near, chosen, slot_weight, pick, weight)
    for copy in loads[2:4]:
        copy.wait()
    for copy in weights:
        copy.start()
    rows_in[...] = dot(pick[...], tok_buf[...], NN).astype(BF)
    pl.semaphore_wait(barrier, len(friends))

    block = lambda n: pl.ds(MOST * n, MOST)

    def dispatch(which, g, src, dst):
        return [
            send(src.at[block(n)], dst.at[block(4 * g + n)], disp_s.at[which, 4 * g + n],
                 disp_r.at[which, 4 * g + n], (near_group if g else group)[n])
            for n in (2, 3, 1, 0) if g or n
        ]

    row_copies = [dispatch(0, 0, rows_in, rows)]
    rows[0:MOST, :] = rows_in[0:MOST, :]
    grads_in[...] = dot(pick[...], grad_buf[...], NN).astype(BF)
    grad_copies = [dispatch(1, 0, grads_in, raw)]
    raw[0:MOST, :] = grads_in[0:MOST, :]

    half = rows.shape[1] // 2
    mine = pl.ds(pl.multiple_of(yl * half, half), half)
    slot = lambda d, g: pl.ds(2 * SLOTS * d + SLOTS * g, SLOTS)
    gap = jnp.zeros((SLOTS, 4), BF)
    blank = jnp.zeros((SLOTS, QPAD - QUARTER), BF)
    early_x, early_g, late_h, late_gu = [], [], [], []

    def early_sends(which, g, src, dst):
        return [
            send(src, dst.at[slot(n, g)], early_s.at[which, 4 * g + n], early_r.at[which, 4 * g + n], ring_a[n])
            for n in (2, 1, 3)
        ]

    def late_sends(which, g, src, dst):
        here = pl.ds(SLOTS * g, SLOTS)
        dst[here, :] = src[a, here, :]
        return [
            send(src.at[(a + n) % 4, here], dst.at[slot(n, g)], late_s.at[which, 4 * g + n],
                 late_r.at[which, 4 * g + n], ring_a[n])
            for n in (2, 1, 3)
        ]

    for g in range(2):
        here = pl.ds(SLOTS * g, SLOTS)
        for copy in row_copies[g]:
            copy.wait_recv()
        if g == 0:
            row_copies.append(dispatch(0, 1, rows_in, rows))
        for which in range(4):
            @pl.when(2 * core + yl == which)
            def _():
                order = [u if which < 2 else 4 * (u % 4) + u // 4 for u in range(16)]
                first = 64 * (which % 2)
                rx[here, :] = jnp.concatenate(
                    [rows[here, 128 * u + first : 128 * u + first + 64] for u in order], axis=1
                )
        early_x += early_sends(0, g, rx.at[here], rx)

        if g == 0:
            for copy in weights[0:4]:
                copy.wait()
        gate_pre = dot(rows[here, :], wg[...], NN)
        up_pre = dot(rows[here, :], wu[...], NN)
        sig = 1.0 / (1.0 + jnp.exp(-gate_pre))
        activated = gate_pre * sig
        ggp[here, :] = (activated * up_pre).astype(BF)
        for which in range(2):
            @pl.when(core == which)
            def _():
                for j in range(4):
                    pieces = []
                    for v in range(8):
                        owner = (v // 2) * 8 + 2 * j + v % 2 if which == 0 else 8 * j + v
                        pieces += [ggp[here, 44 * owner : 44 * owner + 44], gap]
                    hq[j, here, :] = jnp.concatenate(pieces, axis=1)
        late_h += late_sends(0, g, hq, rh)

        for copy in grad_copies[g]:
            copy.wait_recv()
        if g == 0:
            grad_copies.append(dispatch(1, 1, grads_in, raw))
        gout[here, :] = (weight[here, 0:1] * raw[here, :].astype(F32)).astype(BF)
        rg[here, :] = gout[here, mine]
        early_g += early_sends(1, g, rg.at[here], rg)
        if g == 0:
            for copy in weights[4:6]:
                copy.wait()
        grad_hidden = dot(gout[here, :], wd[...], NT)
        gup[here, :] = (grad_hidden * activated).astype(BF)
        ggp[here, :] = (grad_hidden * up_pre * (sig * (1.0 + gate_pre * (1.0 - sig)))).astype(BF)
        for j in range(4):
            columns = slice(QUARTER * j, QUARTER * (j + 1))
            gq[j, here, :] = jnp.concatenate([gup[here, columns], blank, ggp[here, columns], blank], axis=1)
        late_gu += late_sends(1, g, gq, rgu)

    chunk = half // 4
    sums = [[], [], []]
    for copy in early_g + late_h:
        copy.wait_recv()
    part_d[...] = dot(rh[...], rg[...], TN).astype(BF)
    rows_d = QPAD // 4
    for n in (2, 1, 3):
        sums[0].append(send(
            part_d.at[pl.ds(pl.multiple_of((b + n) % 4 * rows_d, rows_d), rows_d)], got_d.at[n],
            sum_s.at[0, n], sum_r.at[0, n], ring_b[n],
        ))
    for copy in early_x + late_gu:
        copy.wait_recv()
    for part in (1, 2):
        for n in (2, 1, 3, 0):
            columns = pl.ds(pl.multiple_of((b + n) % 4 * chunk, chunk), chunk)
            part_gu[part - 1, n] = dot(rx[:, columns], rgu[:, QPAD * (part - 1) : QPAD * part], TN).astype(BF)
            if n:
                sums[part].append(send(
                    part_gu.at[part - 1, n], got_gu.at[part - 1, n],
                    sum_s.at[part, n], sum_r.at[part, n], ring_b[n],
                ))

    slot_grad = dot(ggp[0:SLOTS, :], wg[...], NT) + dot(gup[0:SLOTS, :], wu[...], NT)
    slot_send[...] = slot_grad.astype(BF)
    returns = [
        send(slot_send.at[block(n)], back.at[block(n)], ret_s.at[n], ret_r.at[n], (dp, (me + 4 - n) % 4))
        for n in (2, 1, 3)
    ]
    back[0:MOST, :] = slot_send[0:MOST, :]

    scale = 1.0 / 32
    for copy in sums[0]:
        copy.wait_recv()
    total = part_d[pl.ds(pl.multiple_of(b * rows_d, rows_d), rows_d), :].astype(F32)
    for n in range(1, 4):
        total = total + got_d[n].astype(F32)
    out_d[...] = (total * scale).astype(BF).reshape(out_d.shape)
    put_d = send(out_d.at[1 - yl], land_d.at[yl], put_s.at[0, 0], put_r.at[0, 0], across)
    land_d[yl] = out_d[yl]
    for copy in returns:
        copy.wait_recv()
    for n in range(4):
        part = pl.ds(128 * n, 128)
        token_grad[part, :] = dot(pick[:, part], back[...], TN).astype(BF)
    for part in (1, 2):
        for copy in sums[part]:
            copy.wait_recv()
        total = part_gu[part - 1, 0].astype(F32)
        for n in range(1, 4):
            total = total + got_gu[part - 1, n].astype(F32)
        out_gu[part - 1] = (total * scale).astype(BF).reshape(out_gu.shape[1:])
        for n in (2, 1, 3):
            send(out_gu.at[part - 1, (a + n) % 4], land_gu.at[part - 1, a], put_s.at[part, n],
                 put_r.at[part, n], ring_a[n])
        land_gu[part - 1, a] = out_gu[part - 1, a]

    pltpu.make_async_copy(land_d.at[1 - yl], land_d.at[1 - yl], put_r.at[0, 0]).wait()
    for y in range(2):
        grad_down[0, :, half * y : half * (y + 1)] = land_d[y, 0:44, :]
    for part, dst in ((1, grad_up), (2, grad_gate)):
        for n in (1, 2, 3):
            there = land_gu.at[part - 1, (a + 4 - n) % 4]
            pltpu.make_async_copy(there, there, put_r.at[part, n]).wait()
        for j in range(4):
            dst[0, :, QUARTER * j : QUARTER * (j + 1)] = land_gu[part - 1, j, :, 0:QUARTER]
    for copy in started:
        copy.wait_send()


def main_pass(chosen, slot_weight, tokens, out_grad, w_gate, w_up, w_down):
    width = tokens.shape[1]
    hid = w_gate.shape[2]
    half = width // 2
    chunk = half // 4
    vmem = pl.BlockSpec(memory_space=pltpu.VMEM)
    hbm = pl.BlockSpec(memory_space=pl.ANY)
    dma = pltpu.SemaphoreType.DMA

    def buf(*shape):
        return pltpu.VMEM(shape, BF)

    return pl.pallas_call(
        main_kernel,
        out_shape=(
            pltpu.VMEM(tokens.shape, BF),
            pltpu.VMEM((1, width // 32, hid), BF),
            pltpu.VMEM((1, width // 32, hid), BF),
            pltpu.VMEM((1, hid // 32, width), BF),
        ),
        in_specs=[hbm] * 7,
        out_specs=(vmem,) * 4,
        scratch_shapes=[
            pltpu.VMEM(chosen.shape, jnp.int32), pltpu.VMEM(slot_weight.shape, F32),
            buf(SLOTS, tokens.shape[0]),
            buf(*tokens.shape), buf(*tokens.shape),
            pltpu.VMEM((2 * SLOTS, 128), F32),
            buf(SLOTS, width), buf(SLOTS, width),
            buf(width, hid), buf(width, hid), buf(hid, width),
            buf(2 * SLOTS, width), buf(2 * SLOTS, width), buf(2 * SLOTS, width),
            buf(8 * SLOTS, half), buf(8 * SLOTS, half),
            buf(8 * SLOTS, QPAD), buf(8 * SLOTS, 2 * QPAD),
            buf(4, 2 * SLOTS, QPAD), buf(4, 2 * SLOTS, 2 * QPAD),
            buf(2 * SLOTS, hid), buf(2 * SLOTS, hid),
            buf(SLOTS, width), buf(SLOTS, width),
            buf(QPAD, half), buf(4, QPAD // 4, half),
            buf(2, 4, chunk, QPAD), buf(2, 4, chunk, QPAD),
            buf(2, 48, half), buf(2, 4, 64, QPAD),
            buf(2, 48, half), buf(2, 4, 64, QPAD),
            dma((4,)), dma((6,)),
            dma((2, 8)), dma((2, 8)),
            dma((2, 8)), dma((2, 8)),
            dma((2, 8)), dma((2, 8)),
            dma((4,)), dma((4,)),
            dma((3, 4)), dma((3, 4)),
            dma((3, 4)), dma((3, 4)),
        ],
        compiler_params=pltpu.CompilerParams(
            collective_id=0, has_side_effects=True, vmem_limit_bytes=56 * 2**20
        ),
    )(chosen, slot_weight, tokens, out_grad, w_gate, w_up, w_down)


def store_kernel(*refs):
    sources, results, sems = refs[0:4], refs[4:8], refs[8]
    copies = [pltpu.make_async_copy(sources[n], results[n], sems.at[n]) for n in range(4)]
    for copy in copies:
        copy.start()
    for copy in copies:
        copy.wait()


def local(tokens, out_grad, chosen, slot_weight, w_gate, w_up, w_down):
    results = main_pass(chosen, slot_weight, tokens, out_grad, w_gate, w_up, w_down)
    return pl.pallas_call(
        store_kernel,
        out_shape=tuple(jax.ShapeDtypeStruct(value.shape, value.dtype) for value in results),
        in_specs=[pl.BlockSpec(memory_space=pltpu.VMEM)] * 4,
        out_specs=(pl.BlockSpec(memory_space=pl.ANY),) * 4,
        scratch_shapes=[pltpu.SemaphoreType.DMA((4,))],
        compiler_params=pltpu.CompilerParams(vmem_limit_bytes=4 * 2**20),
    )(*results)


def solution(mesh):
    return jax.shard_map(
        local,
        mesh=mesh,
        in_specs=(
            P(("dp", "expert"), None),
            P(("dp", "expert"), None),
            P(),
            P("expert", None),
            P("expert", None, None),
            P("expert", None, None),
            P("expert", None, None),
        ),
        out_specs=(
            P(("dp", "expert"), None),
            P("expert", "dp", None),
            P("expert", "dp", None),
            P("expert", "dp", None),
        ),
        check_vma=False,
    )
```

```python
import jax
import jax.numpy as jnp
from jax import lax
from jax.experimental import pallas as pl
from jax.experimental.pallas import tpu as pltpu
from jax.sharding import PartitionSpec as P

MESH = pl.DeviceIdType.MESH
BF = jnp.bfloat16
F32 = jnp.float32
MOST = 16
SLOTS = 64
QUARTER = 352
QPAD = 384
NN = (((1,), (0,)), ((), ()))
NT = (((1,), (1,)), ((), ()))
TN = (((0,), (0,)), ((), ()))


def dot(lhs, rhs, dims):
    return lax.dot_general(lhs, rhs, dims, preferred_element_type=F32)


def indicator(cond):
    return jnp.where(cond, 1.0, 0.0).astype(BF)


def one_hot(entries, rows, tile):
    low = lax.broadcasted_iota(jnp.int32, (128, entries.shape[1]), 0) == (entries & 127)
    return rows == tile, indicator(low)


def ranks(counts):
    size = counts.shape[0]
    upper = indicator(
        lax.broadcasted_iota(jnp.int32, (128, 128), 0) <= lax.broadcasted_iota(jnp.int32, (128, 128), 1)
    )
    running = dot(counts.astype(BF), upper, NN)
    totals = dot(counts.astype(BF), jnp.ones((128, 128), BF), NN)
    left = lax.broadcasted_iota(jnp.int32, (size, size), 0)
    right = lax.broadcasted_iota(jnp.int32, (size, size), 1)
    before = indicator(((left >> 2) == (right >> 2)) & (right < left))
    rank = running + dot(before, totals.astype(BF), NN) - 1.0
    return jnp.where(counts > 0.5, rank, -1.0)


def line(values, n):
    return jnp.concatenate([values[4 * n + h : 4 * n + h + 1, :] for h in range(4)], axis=1)


def route_picks(me, dp, chosen, pick):
    row = lax.broadcasted_iota(jnp.int32, (16, chosen.shape[1]), 0)
    lists = chosen[...]
    counts = jnp.zeros((16, 128), F32)
    for f in range(4):
        entries = lists[f : f + 1, :]
        high = (entries >> 7) - (dp * 4 + me) * 4
        high = jnp.where((high >= 0) & (high < 4), high + 4 * ((f + 4 - me) % 4), -1)
        tile, low = one_hot(entries, row, high)
        counts = counts + dot(indicator(tile), low, NT)
    rank = ranks(counts)
    place = lax.broadcasted_iota(jnp.int32, (MOST, 512), 0).astype(F32)
    for n in range(4):
        pick[16 * n : 16 * n + 16, :] = indicator(place == line(rank, n))


def route_weights(me, dp, near, chosen, slot_weight, weight):
    lists = chosen[...]
    entries = lists[0:1, :]
    for f in range(1, 4):
        entries = jnp.where(me == f, lists[f : f + 1, :], entries)
    row = lax.broadcasted_iota(jnp.int32, (16, chosen.shape[1]), 0)
    wanted = 4 * ((me + 4 - (row >> 2)) & 3) + (row & 3)
    value = slot_weight[...]
    part_a = value.astype(BF).astype(F32)
    part_b = (value - part_a).astype(BF).astype(F32)
    part_c = value - part_a - part_b
    stacked = []
    for part in (jnp.ones_like(value), part_a, part_b, part_c):
        for group in (dp, near):
            hit, low = one_hot(entries, wanted, (entries >> 7) - group * 16)
            stacked.append(jnp.where(hit, part, 0.0).astype(BF))
    found = dot(jnp.concatenate(stacked, axis=0), low, NT)
    weight_map = found[32:64] + found[64:96] + found[96:128]
    rank = ranks(found[0:32])
    place = lax.broadcasted_iota(jnp.int32, (MOST, 512), 0).astype(F32)
    for n in range(8):
        chosen_here = jnp.where(place == line(rank, n), line(weight_map, n), 0.0)
        weight[16 * n : 16 * n + 16, :] = jnp.broadcast_to(
            jnp.sum(chosen_here, axis=1, keepdims=True), (MOST, 128)
        )


def main_kernel(chosen_in, slot_weight_in, tokens, out_grad, w_gate, w_up, w_down,
                token_grad, grad_gate, grad_up, grad_down,
                chosen, slot_weight, pick, tok_buf, grad_buf, weight, rows_in, grads_in, wg, wu, wd,
                rows, raw, gout, rx, rg, rh, rgu, hq, gq, ggp, gup, slot_send, back, part_d, via_d, got_d,
                part_gu, via_gu, got_gu, out_d, out_gu, land_d, land_gu,
                load_sem, w_sem, disp_s, disp_r, early_s, early_r, late_s, late_r,
                ret_s, ret_r, sum_s, sum_r, put_s, put_r):
    dp = lax.axis_index("dp")
    me = lax.axis_index("expert")
    yl = dp % 2
    core = me % 2
    along_x = (dp // 2) % 4
    along_z = dp // 8
    a = along_x + core * (along_z - along_x)
    b = along_z + core * (along_x - along_z)

    def at_dp(a_at, b_at, y_at):
        return a_at * (2 + 6 * core) + b_at * (8 - 6 * core) + y_at

    ring_a = [(at_dp((a + n) % 4, b, yl), me) for n in range(4)]
    ring_b = [(at_dp(a, (b + n) % 4, yl), me) for n in range(4)]
    across = (at_dp(a, b, 1 - yl), me)
    started = []

    def send(src, dst, send_sem, recv_sem, target):
        copy = pltpu.make_async_remote_copy(
            src_ref=src, dst_ref=dst, send_sem=send_sem, recv_sem=recv_sem,
            device_id=target, device_id_type=MESH,
        )
        copy.start()
        started.append(copy)
        return copy

    barrier = pltpu.get_barrier_semaphore()
    near = dp + 1 - 2 * yl
    group = [(dp, (me + n) % 4) for n in range(4)]
    near_group = [(near, (me + n) % 4) for n in range(4)]
    friends = group[1:] + near_group + ring_a[1:] + ring_b[1:]
    for friend in friends:
        pl.semaphore_signal(barrier, inc=1, device_id=friend, device_id_type=MESH)

    loads = [
        pltpu.make_async_copy(src, dst, load_sem.at[n])
        for n, (src, dst) in enumerate(
            ((chosen_in, chosen), (slot_weight_in, slot_weight), (tokens, tok_buf), (out_grad, grad_buf))
        )
    ]
    weights = []
    for n, (src, dst) in enumerate(((w_gate, wg), (w_up, wu), (w_down, wd))):
        middle = dst.shape[0] // 2
        for h in range(2):
            part = pl.ds(h * middle, middle)
            weights.append(pltpu.make_async_copy(src.at[0, part], dst.at[part], w_sem.at[2 * n + h]))
    for copy in loads:
        copy.start()
    loads[0].wait()
    route_picks(me, dp, chosen, pick)
    loads[2].wait()
    rows_in[...] = dot(pick[...], tok_buf[...], NN).astype(BF)
    pl.semaphore_wait(barrier, len(friends))

    block = lambda n: pl.ds(MOST * n, MOST)

    def dispatch(which, g, src, dst):
        return [
            send(src.at[block(n)], dst.at[block(4 * g + n)], disp_s.at[which, 4 * g + n],
                 disp_r.at[which, 4 * g + n], (near_group if g else group)[n])
            for n in (2, 3, 1, 0) if g or n
        ]

    row_copies = [dispatch(0, 0, rows_in, rows)]
    rows[0:MOST, :] = rows_in[0:MOST, :]
    loads[3].wait()
    for copy in weights:
        copy.start()
    grads_in[...] = dot(pick[...], grad_buf[...], NN).astype(BF)
    grad_copies = [dispatch(1, 0, grads_in, raw)]
    raw[0:MOST, :] = grads_in[0:MOST, :]
    loads[1].wait()
    route_weights(me, dp, near, chosen, slot_weight, weight)

    half = rows.shape[1] // 2
    mine = pl.ds(pl.multiple_of(yl * half, half), half)
    slot = lambda d, g: pl.ds(2 * SLOTS * d + SLOTS * g, SLOTS)
    gap = jnp.zeros((SLOTS, 4), BF)
    blank = jnp.zeros((SLOTS, QPAD - QUARTER), BF)
    early_x, early_g, late_h, late_gu = [], [], [], []

    def early_sends(which, g, src, dst):
        return [
            send(src, dst.at[slot(n, g)], early_s.at[which, 4 * g + n], early_r.at[which, 4 * g + n], ring_a[n])
            for n in (2, 1, 3)
        ]

    def late_sends(which, g, src, dst):
        here = pl.ds(SLOTS * g, SLOTS)
        dst[here, :] = src[a, here, :]
        return [
            send(src.at[(a + n) % 4, here], dst.at[slot(n, g)], late_s.at[which, 4 * g + n],
                 late_r.at[which, 4 * g + n], ring_a[n])
            for n in (2, 1, 3)
        ]

    for g in range(2):
        here = pl.ds(SLOTS * g, SLOTS)
        for copy in row_copies[g]:
            copy.wait_recv()
        if g == 0:
            row_copies.append(dispatch(0, 1, rows_in, rows))
        for which in range(4):
            @pl.when(2 * core + yl == which)
            def _():
                order = [u if which < 2 else 4 * (u % 4) + u // 4 for u in range(16)]
                first = 64 * (which % 2)
                rx[here, :] = jnp.concatenate(
                    [rows[here, 128 * u + first : 128 * u + first + 64] for u in order], axis=1
                )
        early_x += early_sends(0, g, rx.at[here], rx)

        if g == 0:
            for copy in weights[0:4]:
                copy.wait()
        gate_pre = dot(rows[here, :], wg[...], NN)
        up_pre = dot(rows[here, :], wu[...], NN)
        sig = 1.0 / (1.0 + jnp.exp(-gate_pre))
        activated = gate_pre * sig
        ggp[here, :] = (activated * up_pre).astype(BF)
        for which in range(2):
            @pl.when(core == which)
            def _():
                for j in range(4):
                    pieces = []
                    for v in range(8):
                        owner = (v // 2) * 8 + 2 * j + v % 2 if which == 0 else 8 * j + v
                        pieces += [ggp[here, 44 * owner : 44 * owner + 44], gap]
                    hq[j, here, :] = jnp.concatenate(pieces, axis=1)
        late_h += late_sends(0, g, hq, rh)

        for copy in grad_copies[g]:
            copy.wait_recv()
        if g == 0:
            grad_copies.append(dispatch(1, 1, grads_in, raw))
        gout[here, :] = (weight[here, 0:1] * raw[here, :].astype(F32)).astype(BF)
        rg[here, :] = gout[here, mine]
        early_g += early_sends(1, g, rg.at[here], rg)
        if g == 0:
            for copy in weights[4:6]:
                copy.wait()
        grad_hidden = dot(gout[here, :], wd[...], NT)
        gup[here, :] = (grad_hidden * activated).astype(BF)
        ggp[here, :] = (grad_hidden * up_pre * (sig * (1.0 + gate_pre * (1.0 - sig)))).astype(BF)
        for j in range(4):
            columns = slice(QUARTER * j, QUARTER * (j + 1))
            gq[j, here, :] = jnp.concatenate([gup[here, columns], blank, ggp[here, columns], blank], axis=1)
        late_gu += late_sends(1, g, gq, rgu)

    chunk = half // 4
    rows_d = QPAD // 4

    def far_sends(part, first, second, dst):
        return [
            send(first, dst.at[0], sum_s.at[part, 0], sum_r.at[part, 0], ring_b[1]),
            send(second, dst.at[1], sum_s.at[part, 2], sum_r.at[part, 2], ring_b[3]),
        ]

    def near_sends(part, after, before, dst):
        return [
            send(after, dst.at[0], sum_s.at[part, 1], sum_r.at[part, 1], ring_b[1]),
            send(before, dst.at[1], sum_s.at[part, 3], sum_r.at[part, 3], ring_b[3]),
        ]

    def tile_gu(part, n):
        columns = pl.ds(pl.multiple_of((b + n) % 4 * chunk, chunk), chunk)
        part_gu[part - 1, n] = dot(rx[:, columns], rgu[:, QPAD * (part - 1) : QPAD * part], TN).astype(BF)

    def rows_at(n, h):
        step = rows_d // 2
        return pl.ds(pl.multiple_of((b + n) % 4 * rows_d, rows_d) + h * step, step)

    for copy in early_g + late_h:
        copy.wait_recv()
    part_d[...] = dot(rh[...], rg[...], TN).astype(BF)
    relays = [far_sends(0, part_d.at[rows_at(2, 0)], part_d.at[rows_at(2, 1)], via_d)]
    for copy in early_x + late_gu:
        copy.wait_recv()
    middle = chunk // 2
    for part in (1, 2):
        tile_gu(part, 2)
        far = part_gu.at[part - 1, 2]
        relays.append(far_sends(part, far.at[0:middle], far.at[middle:chunk], via_gu.at[part - 1]))
    tile_gu(1, 1)
    tile_gu(1, 3)
    sums = []
    for copy in relays[0]:
        copy.wait_recv()
    for n, h in ((1, 0), (3, 1)):
        part_d[rows_at(n, h), :] = (part_d[rows_at(n, h), :].astype(F32) + via_d[h].astype(F32)).astype(BF)
    whole = lambda n: pl.ds(pl.multiple_of((b + n) % 4 * rows_d, rows_d), rows_d)
    sums.append(near_sends(0, part_d.at[whole(1)], part_d.at[whole(3)], got_d))
    tile_gu(2, 1)
    tile_gu(2, 3)
    for part in (1, 2):
        for copy in relays[part]:
            copy.wait_recv()
        for n, h in ((1, 0), (3, 1)):
            rows_h = pl.ds(middle * h, middle)
            part_gu[part - 1, n, rows_h, :] = (
                part_gu[part - 1, n, rows_h, :].astype(F32) + via_gu[part - 1, h].astype(F32)
            ).astype(BF)
        sums.append(near_sends(part, part_gu.at[part - 1, 1], part_gu.at[part - 1, 3], got_gu.at[part - 1]))
    tile_gu(1, 0)
    tile_gu(2, 0)

    slot_grad = dot(ggp[0:SLOTS, :], wg[...], NT) + dot(gup[0:SLOTS, :], wu[...], NT)
    slot_send[...] = slot_grad.astype(BF)
    returns = [
        send(slot_send.at[block(n)], back.at[block(n)], ret_s.at[n], ret_r.at[n], (dp, (me + 4 - n) % 4))
        for n in (2, 1, 3)
    ]
    back[0:MOST, :] = slot_send[0:MOST, :]

    scale = 1.0 / 32
    for copy in sums[0]:
        copy.wait_recv()
    total = part_d[pl.ds(pl.multiple_of(b * rows_d, rows_d), rows_d), :].astype(F32)
    for n in range(2):
        total = total + got_d[n].astype(F32)
    out_d[...] = (total * scale).astype(BF).reshape(out_d.shape)
    put_d = send(out_d.at[1 - yl], land_d.at[yl], put_s.at[0, 0], put_r.at[0, 0], across)
    land_d[yl] = out_d[yl]
    for part in (1, 2):
        for copy in sums[part]:
            copy.wait_recv()
        total = part_gu[part - 1, 0].astype(F32)
        for n in range(2):
            total = total + got_gu[part - 1, n].astype(F32)
        out_gu[part - 1] = (total * scale).astype(BF).reshape(out_gu.shape[1:])
        for n in (2, 1, 3):
            send(out_gu.at[part - 1, (a + n) % 4], land_gu.at[part - 1, a], put_s.at[part, n],
                 put_r.at[part, n], ring_a[n])
        land_gu[part - 1, a] = out_gu[part - 1, a]

    for copy in started[:-7]:
        copy.wait_send()
    for copy in returns:
        copy.wait_recv()
    for n in range(4):
        part = pl.ds(128 * n, 128)
        token_grad[part, :] = dot(pick[:, part], back[...], TN).astype(BF)
    pltpu.make_async_copy(land_d.at[1 - yl], land_d.at[1 - yl], put_r.at[0, 0]).wait()
    for y in range(2):
        grad_down[0, :, half * y : half * (y + 1)] = land_d[y, 0:44, :]
    for part, dst in ((1, grad_up), (2, grad_gate)):
        for n in (1, 2, 3):
            there = land_gu.at[part - 1, (a + 4 - n) % 4]
            pltpu.make_async_copy(there, there, put_r.at[part, n]).wait()
        for j in range(4):
            dst[0, :, QUARTER * j : QUARTER * (j + 1)] = land_gu[part - 1, j, :, 0:QUARTER]
    for copy in started[-7:]:
        copy.wait_send()


def main_pass(chosen, slot_weight, tokens, out_grad, w_gate, w_up, w_down):
    width = tokens.shape[1]
    hid = w_gate.shape[2]
    half = width // 2
    chunk = half // 4
    vmem = pl.BlockSpec(memory_space=pltpu.VMEM)
    hbm = pl.BlockSpec(memory_space=pl.ANY)
    dma = pltpu.SemaphoreType.DMA

    def buf(*shape):
        return pltpu.VMEM(shape, BF)

    return pl.pallas_call(
        main_kernel,
        out_shape=(
            pltpu.VMEM(tokens.shape, BF),
            pltpu.VMEM((1, width // 32, hid), BF),
            pltpu.VMEM((1, width // 32, hid), BF),
            pltpu.VMEM((1, hid // 32, width), BF),
        ),
        in_specs=[hbm] * 7,
        out_specs=(vmem,) * 4,
        scratch_shapes=[
            pltpu.VMEM(chosen.shape, jnp.int32), pltpu.VMEM(slot_weight.shape, F32),
            buf(SLOTS, tokens.shape[0]),
            buf(*tokens.shape), buf(*tokens.shape),
            pltpu.VMEM((2 * SLOTS, 128), F32),
            buf(SLOTS, width), buf(SLOTS, width),
            buf(width, hid), buf(width, hid), buf(hid, width),
            buf(2 * SLOTS, width), buf(2 * SLOTS, width), buf(2 * SLOTS, width),
            buf(8 * SLOTS, half), buf(8 * SLOTS, half),
            buf(8 * SLOTS, QPAD), buf(8 * SLOTS, 2 * QPAD),
            buf(4, 2 * SLOTS, QPAD), buf(4, 2 * SLOTS, 2 * QPAD),
            buf(2 * SLOTS, hid), buf(2 * SLOTS, hid),
            buf(SLOTS, width), buf(SLOTS, width),
            buf(QPAD, half), buf(2, QPAD // 8, half), buf(2, QPAD // 4, half),
            buf(2, 4, chunk, QPAD), buf(2, 2, chunk // 2, QPAD), buf(2, 2, chunk, QPAD),
            buf(2, 48, half), buf(2, 4, 64, QPAD),
            buf(2, 48, half), buf(2, 4, 64, QPAD),
            dma((4,)), dma((6,)),
            dma((2, 8)), dma((2, 8)),
            dma((2, 8)), dma((2, 8)),
            dma((2, 8)), dma((2, 8)),
            dma((4,)), dma((4,)),
            dma((3, 4)), dma((3, 4)),
            dma((3, 4)), dma((3, 4)),
        ],
        compiler_params=pltpu.CompilerParams(
            collective_id=0, has_side_effects=True, vmem_limit_bytes=56 * 2**20
        ),
    )(chosen, slot_weight, tokens, out_grad, w_gate, w_up, w_down)


def store_kernel(*refs):
    sources, results, sems = refs[0:4], refs[4:8], refs[8]
    copies = [pltpu.make_async_copy(sources[n], results[n], sems.at[n]) for n in range(4)]
    for copy in copies:
        copy.start()
    for copy in copies:
        copy.wait()


def local(tokens, out_grad, chosen, slot_weight, w_gate, w_up, w_down):
    results = main_pass(chosen, slot_weight, tokens, out_grad, w_gate, w_up, w_down)
    return pl.pallas_call(
        store_kernel,
        out_shape=tuple(jax.ShapeDtypeStruct(value.shape, value.dtype) for value in results),
        in_specs=[pl.BlockSpec(memory_space=pltpu.VMEM)] * 4,
        out_specs=(pl.BlockSpec(memory_space=pl.ANY),) * 4,
        scratch_shapes=[pltpu.SemaphoreType.DMA((4,))],
        compiler_params=pltpu.CompilerParams(vmem_limit_bytes=4 * 2**20),
    )(*results)


def solution(mesh):
    return jax.shard_map(
        local,
        mesh=mesh,
        in_specs=(
            P(("dp", "expert"), None),
            P(("dp", "expert"), None),
            P(),
            P("expert", None),
            P("expert", None, None),
            P("expert", None, None),
            P("expert", None, None),
        ),
        out_specs=(
            P(("dp", "expert"), None),
            P("expert", "dp", None),
            P("expert", "dp", None),
            P("expert", "dp", None),
        ),
        check_vma=False,
    )
```

```python
import jax
import jax.numpy as jnp
from jax import lax
from jax.experimental import pallas as pl
from jax.experimental.pallas import tpu as pltpu
from jax.sharding import PartitionSpec as P

MESH = pl.DeviceIdType.MESH
BF = jnp.bfloat16
F32 = jnp.float32
MOST = 16
SLOTS = 64
QUARTER = 352
QPAD = 384
NN = (((1,), (0,)), ((), ()))
NT = (((1,), (1,)), ((), ()))
TN = (((0,), (0,)), ((), ()))


def dot(lhs, rhs, dims):
    return lax.dot_general(lhs, rhs, dims, preferred_element_type=F32)


def indicator(cond):
    return jnp.where(cond, 1.0, 0.0).astype(BF)


def one_hot(entries, rows, tile):
    low = lax.broadcasted_iota(jnp.int32, (128, entries.shape[1]), 0) == (entries & 127)
    return rows == tile, indicator(low)


def ranks(counts):
    size = counts.shape[0]
    upper = indicator(
        lax.broadcasted_iota(jnp.int32, (128, 128), 0) <= lax.broadcasted_iota(jnp.int32, (128, 128), 1)
    )
    running = dot(counts.astype(BF), upper, NN)
    totals = dot(counts.astype(BF), jnp.ones((128, 128), BF), NN)
    left = lax.broadcasted_iota(jnp.int32, (size, size), 0)
    right = lax.broadcasted_iota(jnp.int32, (size, size), 1)
    before = indicator(((left >> 2) == (right >> 2)) & (right < left))
    rank = running + dot(before, totals.astype(BF), NN) - 1.0
    return jnp.where(counts > 0.5, rank, -1.0)


def line(values, n):
    return jnp.concatenate([values[4 * n + h : 4 * n + h + 1, :] for h in range(4)], axis=1)


def route_picks(me, dp, chosen, pick):
    row = lax.broadcasted_iota(jnp.int32, (16, chosen.shape[1]), 0)
    lists = chosen[...]
    counts = jnp.zeros((16, 128), F32)
    for f in range(4):
        entries = lists[f : f + 1, :]
        high = (entries >> 7) - (dp * 4 + me) * 4
        high = jnp.where((high >= 0) & (high < 4), high + 4 * ((f + 4 - me) % 4), -1)
        tile, low = one_hot(entries, row, high)
        counts = counts + dot(indicator(tile), low, NT)
    rank = ranks(counts)
    place = lax.broadcasted_iota(jnp.int32, (MOST, 512), 0).astype(F32)
    for n in range(4):
        pick[16 * n : 16 * n + 16, :] = indicator(place == line(rank, n))


def route_weights(me, dp, near, chosen, slot_weight, weight):
    lists = chosen[...]
    entries = lists[0:1, :]
    for f in range(1, 4):
        entries = jnp.where(me == f, lists[f : f + 1, :], entries)
    row = lax.broadcasted_iota(jnp.int32, (16, chosen.shape[1]), 0)
    wanted = 4 * ((me + 4 - (row >> 2)) & 3) + (row & 3)
    value = slot_weight[...]
    part_a = value.astype(BF).astype(F32)
    part_b = (value - part_a).astype(BF).astype(F32)
    part_c = value - part_a - part_b
    stacked = []
    for part in (jnp.ones_like(value), part_a, part_b, part_c):
        for group in (dp, near):
            hit, low = one_hot(entries, wanted, (entries >> 7) - group * 16)
            stacked.append(jnp.where(hit, part, 0.0).astype(BF))
    found = dot(jnp.concatenate(stacked, axis=0), low, NT)
    weight_map = found[32:64] + found[64:96] + found[96:128]
    rank = ranks(found[0:32])
    place = lax.broadcasted_iota(jnp.int32, (MOST, 512), 0).astype(F32)
    for n in range(8):
        chosen_here = jnp.where(place == line(rank, n), line(weight_map, n), 0.0)
        weight[16 * n : 16 * n + 16, :] = jnp.broadcast_to(
            jnp.sum(chosen_here, axis=1, keepdims=True), (MOST, 128)
        )


def main_kernel(chosen_in, slot_weight_in, tokens, out_grad, w_gate, w_up, w_down,
                token_grad, grad_gate, grad_up, grad_down,
                chosen, slot_weight, pick, tok_buf, grad_buf, weight, rows_in, grads_in, wg, wu, wd,
                rows, raw, gout, rx, rg, rh, rgu, hq, gq, ggp, gup, slot_send, back, part_d, via_d, got_d,
                part_gu, via_gu, got_gu, out_d, out_gu, land_d, land_gu,
                load_sem, w_sem, disp_s, disp_r, early_s, early_r, late_s, late_r,
                ret_s, ret_r, sum_s, sum_r, put_s, put_r):
    dp = lax.axis_index("dp")
    me = lax.axis_index("expert")
    yl = dp % 2
    core = me % 2
    along_x = (dp // 2) % 4
    along_z = dp // 8
    a = along_x + core * (along_z - along_x)
    b = along_z + core * (along_x - along_z)

    def at_dp(a_at, b_at, y_at):
        return a_at * (2 + 6 * core) + b_at * (8 - 6 * core) + y_at

    ring_a = [(at_dp((a + n) % 4, b, yl), me) for n in range(4)]
    ring_b = [(at_dp(a, (b + n) % 4, yl), me) for n in range(4)]
    across = (at_dp(a, b, 1 - yl), me)
    started = []

    def send(src, dst, send_sem, recv_sem, target):
        copy = pltpu.make_async_remote_copy(
            src_ref=src, dst_ref=dst, send_sem=send_sem, recv_sem=recv_sem,
            device_id=target, device_id_type=MESH,
        )
        copy.start()
        started.append(copy)
        return copy

    barrier = pltpu.get_barrier_semaphore()
    near = dp + 1 - 2 * yl
    group = [(dp, (me + n) % 4) for n in range(4)]
    near_group = [(near, (me + n) % 4) for n in range(4)]
    friends = group[1:] + near_group + ring_a[1:] + ring_b[1:]
    for friend in friends:
        pl.semaphore_signal(barrier, inc=1, device_id=friend, device_id_type=MESH)

    loads = [
        pltpu.make_async_copy(src, dst, load_sem.at[n])
        for n, (src, dst) in enumerate(
            ((chosen_in, chosen), (slot_weight_in, slot_weight), (tokens, tok_buf), (out_grad, grad_buf))
        )
    ]
    weights = []
    for n, (src, dst) in enumerate(((w_gate, wg), (w_up, wu), (w_down, wd))):
        middle = dst.shape[0] // 2
        for h in range(2):
            part = pl.ds(h * middle, middle)
            weights.append(pltpu.make_async_copy(src.at[0, part], dst.at[part], w_sem.at[2 * n + h]))
    for copy in loads:
        copy.start()
    loads[0].wait()
    route_picks(me, dp, chosen, pick)
    loads[2].wait()
    rows_in[...] = dot(pick[...], tok_buf[...], NN).astype(BF)
    pl.semaphore_wait(barrier, len(friends))

    block = lambda n: pl.ds(MOST * n, MOST)

    def dispatch(which, g, src, dst):
        return [
            send(src.at[block(n)], dst.at[block(4 * g + n)], disp_s.at[which, 4 * g + n],
                 disp_r.at[which, 4 * g + n], (near_group if g else group)[n])
            for n in (2, 3, 1, 0) if g or n
        ]

    row_copies = [dispatch(0, 0, rows_in, rows)]
    rows[0:MOST, :] = rows_in[0:MOST, :]
    loads[1].wait()
    route_weights(me, dp, near, chosen, slot_weight, weight)
    loads[3].wait()
    for copy in weights:
        copy.start()
    grads_in[...] = dot(pick[...], grad_buf[...], NN).astype(BF)
    grad_copies = [dispatch(1, 0, grads_in, raw)]
    raw[0:MOST, :] = grads_in[0:MOST, :]

    half = rows.shape[1] // 2
    mine = pl.ds(pl.multiple_of(yl * half, half), half)
    slot = lambda d, g: pl.ds(2 * SLOTS * d + SLOTS * g, SLOTS)
    gap = jnp.zeros((SLOTS, 4), BF)
    blank = jnp.zeros((SLOTS, QPAD - QUARTER), BF)
    x_copies, g_copies, late_h, late_gu = [], [], [], []

    def early_sends(which, g, src, dst, reach):
        return [
            send(src, dst.at[slot(n, g)], early_s.at[which, 4 * g + n], early_r.at[which, 4 * g + n], ring_a[n])
            for n in reach
        ]

    def early_forward(which, g, copies, dst):
        for copy in copies:
            copy.wait_recv()
        middle = SLOTS // 2
        forwards = []
        for h, n in ((0, 1), (1, 3)):
            there = lambda d: pl.ds(2 * SLOTS * d + SLOTS * g + middle * h, middle)
            forwards.append(send(
                dst.at[there(n)], dst.at[there(2)], early_s.at[which, 4 * g + 2 * h],
                early_r.at[which, 4 * g + 2 * h], ring_a[n],
            ))
        return forwards

    def late_sends(which, g, src, dst):
        here = pl.ds(SLOTS * g, SLOTS)
        dst[here, :] = src[a, here, :]
        return [
            send(src.at[(a + n) % 4, here], dst.at[slot(n, g)], late_s.at[which, 4 * g + n],
                 late_r.at[which, 4 * g + n], ring_a[n])
            for n in (2, 1, 3)
        ]

    for g in range(2):
        here = pl.ds(SLOTS * g, SLOTS)
        for copy in row_copies[g]:
            copy.wait_recv()
        if g == 0:
            row_copies.append(dispatch(0, 1, rows_in, rows))
        for which in range(4):
            @pl.when(2 * core + yl == which)
            def _():
                order = [u if which < 2 else 4 * (u % 4) + u // 4 for u in range(16)]
                first = 64 * (which % 2)
                rx[here, :] = jnp.concatenate(
                    [rows[here, 128 * u + first : 128 * u + first + 64] for u in order], axis=1
                )
        x_copies.append(early_sends(0, g, rx.at[here], rx, (1, 3)))

        if g == 0:
            for copy in weights[0:4]:
                copy.wait()
        gate_pre = dot(rows[here, :], wg[...], NN)
        up_pre = dot(rows[here, :], wu[...], NN)
        sig = 1.0 / (1.0 + jnp.exp(-gate_pre))
        activated = gate_pre * sig
        ggp[here, :] = (activated * up_pre).astype(BF)
        for which in range(2):
            @pl.when(core == which)
            def _():
                for j in range(4):
                    pieces = []
                    for v in range(8):
                        owner = (v // 2) * 8 + 2 * j + v % 2 if which == 0 else 8 * j + v
                        pieces += [ggp[here, 44 * owner : 44 * owner + 44], gap]
                    hq[j, here, :] = jnp.concatenate(pieces, axis=1)
        late_h += late_sends(0, g, hq, rh)

        for copy in grad_copies[g]:
            copy.wait_recv()
        if g == 0:
            grad_copies.append(dispatch(1, 1, grads_in, raw))
        gout[here, :] = (weight[here, 0:1] * raw[here, :].astype(F32)).astype(BF)
        rg[here, :] = gout[here, mine]
        g_copies.append(early_sends(1, g, rg.at[here], rg, (2, 1, 3) if g else (1, 3)))
        if g == 0:
            for copy in weights[4:6]:
                copy.wait()
        grad_hidden = dot(gout[here, :], wd[...], NT)
        gup[here, :] = (grad_hidden * activated).astype(BF)
        ggp[here, :] = (grad_hidden * up_pre * (sig * (1.0 + gate_pre * (1.0 - sig)))).astype(BF)
        for j in range(4):
            columns = slice(QUARTER * j, QUARTER * (j + 1))
            gq[j, here, :] = jnp.concatenate([gup[here, columns], blank, ggp[here, columns], blank], axis=1)
        late_gu += late_sends(1, g, gq, rgu)

    early_g = early_forward(1, 0, g_copies[0], rg) + g_copies[1]
    early_x = early_forward(0, 0, x_copies[0], rx) + early_forward(0, 1, x_copies[1], rx)

    slot_grad = dot(ggp[0:SLOTS, :], wg[...], NT) + dot(gup[0:SLOTS, :], wu[...], NT)
    slot_send[...] = slot_grad.astype(BF)
    returns = [
        send(slot_send.at[block(n)], back.at[block(n)], ret_s.at[n], ret_r.at[n], (dp, (me + 4 - n) % 4))
        for n in (2, 1, 3)
    ]
    back[0:MOST, :] = slot_send[0:MOST, :]

    chunk = half // 4
    rows_d = QPAD // 4

    def far_sends(part, first, second, dst):
        return [
            send(first, dst.at[0], sum_s.at[part, 0], sum_r.at[part, 0], ring_b[1]),
            send(second, dst.at[1], sum_s.at[part, 2], sum_r.at[part, 2], ring_b[3]),
        ]

    def near_sends(part, after, before, dst):
        return [
            send(after, dst.at[0], sum_s.at[part, 1], sum_r.at[part, 1], ring_b[1]),
            send(before, dst.at[1], sum_s.at[part, 3], sum_r.at[part, 3], ring_b[3]),
        ]

    def tile_gu(part, n):
        columns = pl.ds(pl.multiple_of((b + n) % 4 * chunk, chunk), chunk)
        part_gu[part - 1, n] = dot(rx[:, columns], rgu[:, QPAD * (part - 1) : QPAD * part], TN).astype(BF)

    def rows_at(n, h):
        step = rows_d // 2
        return pl.ds(pl.multiple_of((b + n) % 4 * rows_d, rows_d) + h * step, step)

    for copy in early_g + late_h:
        copy.wait_recv()
    part_d[...] = dot(rh[...], rg[...], TN).astype(BF)
    relays = [far_sends(0, part_d.at[rows_at(2, 0)], part_d.at[rows_at(2, 1)], via_d)]
    for copy in early_x + late_gu:
        copy.wait_recv()
    middle = chunk // 2
    for part in (1, 2):
        tile_gu(part, 2)
        far = part_gu.at[part - 1, 2]
        relays.append(far_sends(part, far.at[0:middle], far.at[middle:chunk], via_gu.at[part - 1]))
    tile_gu(1, 1)
    tile_gu(1, 3)
    sums = []
    for copy in relays[0]:
        copy.wait_recv()
    for n, h in ((1, 0), (3, 1)):
        part_d[rows_at(n, h), :] = (part_d[rows_at(n, h), :].astype(F32) + via_d[h].astype(F32)).astype(BF)
    whole = lambda n: pl.ds(pl.multiple_of((b + n) % 4 * rows_d, rows_d), rows_d)
    sums.append(near_sends(0, part_d.at[whole(1)], part_d.at[whole(3)], got_d))
    tile_gu(2, 1)
    tile_gu(2, 3)
    for part in (1, 2):
        for copy in relays[part]:
            copy.wait_recv()
        for n, h in ((1, 0), (3, 1)):
            rows_h = pl.ds(middle * h, middle)
            part_gu[part - 1, n, rows_h, :] = (
                part_gu[part - 1, n, rows_h, :].astype(F32) + via_gu[part - 1, h].astype(F32)
            ).astype(BF)
        sums.append(near_sends(part, part_gu.at[part - 1, 1], part_gu.at[part - 1, 3], got_gu.at[part - 1]))
    tile_gu(1, 0)
    tile_gu(2, 0)

    scale = 1.0 / 32
    for copy in sums[0]:
        copy.wait_recv()
    total = part_d[pl.ds(pl.multiple_of(b * rows_d, rows_d), rows_d), :].astype(F32)
    for n in range(2):
        total = total + got_d[n].astype(F32)
    out_d[...] = (total * scale).astype(BF).reshape(out_d.shape)
    put_d = send(out_d.at[1 - yl], land_d.at[yl], put_s.at[0, 0], put_r.at[0, 0], across)
    land_d[yl] = out_d[yl]
    for part in (1, 2):
        for copy in sums[part]:
            copy.wait_recv()
        total = part_gu[part - 1, 0].astype(F32)
        for n in range(2):
            total = total + got_gu[part - 1, n].astype(F32)
        out_gu[part - 1] = (total * scale).astype(BF).reshape(out_gu.shape[1:])
        for n in (2, 1, 3):
            send(out_gu.at[part - 1, (a + n) % 4], land_gu.at[part - 1, a], put_s.at[part, n],
                 put_r.at[part, n], ring_a[n])
        land_gu[part - 1, a] = out_gu[part - 1, a]

    for copy in started[:-7]:
        copy.wait_send()
    for copy in returns:
        copy.wait_recv()
    for n in range(4):
        part = pl.ds(128 * n, 128)
        token_grad[part, :] = dot(pick[:, part], back[...], TN).astype(BF)
    pltpu.make_async_copy(land_d.at[1 - yl], land_d.at[1 - yl], put_r.at[0, 0]).wait()
    for y in range(2):
        grad_down[0, :, half * y : half * (y + 1)] = land_d[y, 0:44, :]
    for part, dst in ((1, grad_up), (2, grad_gate)):
        for n in (1, 2, 3):
            there = land_gu.at[part - 1, (a + 4 - n) % 4]
            pltpu.make_async_copy(there, there, put_r.at[part, n]).wait()
        for j in range(4):
            dst[0, :, QUARTER * j : QUARTER * (j + 1)] = land_gu[part - 1, j, :, 0:QUARTER]
    for copy in started[-7:]:
        copy.wait_send()


def main_pass(chosen, slot_weight, tokens, out_grad, w_gate, w_up, w_down):
    width = tokens.shape[1]
    hid = w_gate.shape[2]
    half = width // 2
    chunk = half // 4
    vmem = pl.BlockSpec(memory_space=pltpu.VMEM)
    hbm = pl.BlockSpec(memory_space=pl.ANY)
    dma = pltpu.SemaphoreType.DMA

    def buf(*shape):
        return pltpu.VMEM(shape, BF)

    return pl.pallas_call(
        main_kernel,
        out_shape=(
            pltpu.VMEM(tokens.shape, BF),
            pltpu.VMEM((1, width // 32, hid), BF),
            pltpu.VMEM((1, width // 32, hid), BF),
            pltpu.VMEM((1, hid // 32, width), BF),
        ),
        in_specs=[hbm] * 7,
        out_specs=(vmem,) * 4,
        scratch_shapes=[
            pltpu.VMEM(chosen.shape, jnp.int32), pltpu.VMEM(slot_weight.shape, F32),
            buf(SLOTS, tokens.shape[0]),
            buf(*tokens.shape), buf(*tokens.shape),
            pltpu.VMEM((2 * SLOTS, 128), F32),
            buf(SLOTS, width), buf(SLOTS, width),
            buf(width, hid), buf(width, hid), buf(hid, width),
            buf(2 * SLOTS, width), buf(2 * SLOTS, width), buf(2 * SLOTS, width),
            buf(8 * SLOTS, half), buf(8 * SLOTS, half),
            buf(8 * SLOTS, QPAD), buf(8 * SLOTS, 2 * QPAD),
            buf(4, 2 * SLOTS, QPAD), buf(4, 2 * SLOTS, 2 * QPAD),
            buf(2 * SLOTS, hid), buf(2 * SLOTS, hid),
            buf(SLOTS, width), buf(SLOTS, width),
            buf(QPAD, half), buf(2, QPAD // 8, half), buf(2, QPAD // 4, half),
            buf(2, 4, chunk, QPAD), buf(2, 2, chunk // 2, QPAD), buf(2, 2, chunk, QPAD),
            buf(2, 48, half), buf(2, 4, 64, QPAD),
            buf(2, 48, half), buf(2, 4, 64, QPAD),
            dma((4,)), dma((6,)),
            dma((2, 8)), dma((2, 8)),
            dma((2, 8)), dma((2, 8)),
            dma((2, 8)), dma((2, 8)),
            dma((4,)), dma((4,)),
            dma((3, 4)), dma((3, 4)),
            dma((3, 4)), dma((3, 4)),
        ],
        compiler_params=pltpu.CompilerParams(
            collective_id=0, has_side_effects=True, vmem_limit_bytes=56 * 2**20
        ),
    )(chosen, slot_weight, tokens, out_grad, w_gate, w_up, w_down)


def store_kernel(*refs):
    sources, results, sems = refs[0:4], refs[4:8], refs[8]
    pieces = 4
    size = sources[0].shape[0] // pieces
    copies = [pltpu.make_async_copy(sources[n], results[n], sems.at[n]) for n in range(1, 4)]
    for k in range(pieces):
        part = pl.ds(size * k, size)
        copies.append(pltpu.make_async_copy(sources[0].at[part], results[0].at[part], sems.at[4 + k]))
    for copy in copies:
        copy.start()
    for copy in copies:
        copy.wait()


def local(tokens, out_grad, chosen, slot_weight, w_gate, w_up, w_down):
    results = main_pass(chosen, slot_weight, tokens, out_grad, w_gate, w_up, w_down)
    return pl.pallas_call(
        store_kernel,
        out_shape=tuple(jax.ShapeDtypeStruct(value.shape, value.dtype) for value in results),
        in_specs=[pl.BlockSpec(memory_space=pltpu.VMEM)] * 4,
        out_specs=(pl.BlockSpec(memory_space=pl.ANY),) * 4,
        scratch_shapes=[pltpu.SemaphoreType.DMA((8,))],
        compiler_params=pltpu.CompilerParams(vmem_limit_bytes=4 * 2**20),
    )(*results)


def solution(mesh):
    return jax.shard_map(
        local,
        mesh=mesh,
        in_specs=(
            P(("dp", "expert"), None),
            P(("dp", "expert"), None),
            P(),
            P("expert", None),
            P("expert", None, None),
            P("expert", None, None),
            P("expert", None, None),
        ),
        out_specs=(
            P(("dp", "expert"), None),
            P("expert", "dp", None),
            P("expert", "dp", None),
            P("expert", "dp", None),
        ),
        check_vma=False,
    )
```

```python
import jax
import jax.numpy as jnp
from jax import lax
from jax.experimental import pallas as pl
from jax.experimental.pallas import tpu as pltpu
from jax.sharding import PartitionSpec as P

MESH = pl.DeviceIdType.MESH
BF = jnp.bfloat16
F32 = jnp.float32
MOST = 16
SLOTS = 64
QUARTER = 352
QPAD = 384
NN = (((1,), (0,)), ((), ()))
NT = (((1,), (1,)), ((), ()))
TN = (((0,), (0,)), ((), ()))


def dot(lhs, rhs, dims):
    return lax.dot_general(lhs, rhs, dims, preferred_element_type=F32)


def indicator(cond):
    return jnp.where(cond, 1.0, 0.0).astype(BF)


def one_hot(entries, rows, tile):
    low = lax.broadcasted_iota(jnp.int32, (128, entries.shape[1]), 0) == (entries & 127)
    return rows == tile, indicator(low)


def ranks(counts):
    size = counts.shape[0]
    upper = indicator(
        lax.broadcasted_iota(jnp.int32, (128, 128), 0) <= lax.broadcasted_iota(jnp.int32, (128, 128), 1)
    )
    running = dot(counts.astype(BF), upper, NN)
    totals = dot(counts.astype(BF), jnp.ones((128, 128), BF), NN)
    left = lax.broadcasted_iota(jnp.int32, (size, size), 0)
    right = lax.broadcasted_iota(jnp.int32, (size, size), 1)
    before = indicator(((left >> 2) == (right >> 2)) & (right < left))
    rank = running + dot(before, totals.astype(BF), NN) - 1.0
    return jnp.where(counts > 0.5, rank, -1.0)


def line(values, n):
    return jnp.concatenate([values[4 * n + h : 4 * n + h + 1, :] for h in range(4)], axis=1)


def route_picks(me, dp, chosen, pick):
    row = lax.broadcasted_iota(jnp.int32, (16, chosen.shape[1]), 0)
    lists = chosen[...]
    counts = jnp.zeros((16, 128), F32)
    for f in range(4):
        entries = lists[f : f + 1, :]
        high = (entries >> 7) - (dp * 4 + me) * 4
        high = jnp.where((high >= 0) & (high < 4), high + 4 * ((f + 4 - me) % 4), -1)
        tile, low = one_hot(entries, row, high)
        counts = counts + dot(indicator(tile), low, NT)
    rank = ranks(counts)
    place = lax.broadcasted_iota(jnp.int32, (MOST, 512), 0).astype(F32)
    for n in range(4):
        pick[16 * n : 16 * n + 16, :] = indicator(place == line(rank, n))


def route_weights(me, dp, near, chosen, slot_weight, weight):
    lists = chosen[...]
    entries = lists[0:1, :]
    for f in range(1, 4):
        entries = jnp.where(me == f, lists[f : f + 1, :], entries)
    row = lax.broadcasted_iota(jnp.int32, (16, chosen.shape[1]), 0)
    wanted = 4 * ((me + 4 - (row >> 2)) & 3) + (row & 3)
    value = slot_weight[...]
    part_a = value.astype(BF).astype(F32)
    part_b = (value - part_a).astype(BF).astype(F32)
    part_c = value - part_a - part_b
    stacked = []
    for part in (jnp.ones_like(value), part_a, part_b, part_c):
        for group in (dp, near):
            hit, low = one_hot(entries, wanted, (entries >> 7) - group * 16)
            stacked.append(jnp.where(hit, part, 0.0).astype(BF))
    found = dot(jnp.concatenate(stacked, axis=0), low, NT)
    weight_map = found[32:64] + found[64:96] + found[96:128]
    rank = ranks(found[0:32])
    place = lax.broadcasted_iota(jnp.int32, (MOST, 512), 0).astype(F32)
    for n in range(8):
        chosen_here = jnp.where(place == line(rank, n), line(weight_map, n), 0.0)
        weight[16 * n : 16 * n + 16, :] = jnp.broadcast_to(
            jnp.sum(chosen_here, axis=1, keepdims=True), (MOST, 128)
        )


def main_kernel(chosen_in, slot_weight_in, tokens, out_grad, w_gate, w_up, w_down,
                token_grad, grad_gate, grad_up, grad_down,
                chosen, slot_weight, pick, tok_buf, grad_buf, weight, rows_in, grads_in, wg, wu, wd,
                rows, raw, gout, rx, rg, rh, rgu, hq, gq, ggp, gup, slot_send, back, part_d, via_d, got_d,
                part_gu, via_gu, got_gu, out_d, out_gu, land_d, land_gu,
                load_sem, w_sem, disp_s, disp_r, early_s, early_r, late_s, late_r,
                ret_s, ret_r, sum_s, sum_r, put_s, put_r):
    dp = lax.axis_index("dp")
    me = lax.axis_index("expert")
    yl = dp % 2
    core = me % 2
    along_x = (dp // 2) % 4
    along_z = dp // 8
    a = along_x + core * (along_z - along_x)
    b = along_z + core * (along_x - along_z)

    def at_dp(a_at, b_at, y_at):
        return a_at * (2 + 6 * core) + b_at * (8 - 6 * core) + y_at

    ring_a = [(at_dp((a + n) % 4, b, yl), me) for n in range(4)]
    ring_b = [(at_dp(a, (b + n) % 4, yl), me) for n in range(4)]
    across = (at_dp(a, b, 1 - yl), me)
    started = []

    def send(src, dst, send_sem, recv_sem, target):
        copy = pltpu.make_async_remote_copy(
            src_ref=src, dst_ref=dst, send_sem=send_sem, recv_sem=recv_sem,
            device_id=target, device_id_type=MESH,
        )
        copy.start()
        started.append(copy)
        return copy

    barrier = pltpu.get_barrier_semaphore()
    near = dp + 1 - 2 * yl
    group = [(dp, (me + n) % 4) for n in range(4)]
    near_group = [(near, (me + n) % 4) for n in range(4)]
    friends = group[1:] + near_group + ring_a[1:] + ring_b[1:]
    for friend in friends:
        pl.semaphore_signal(barrier, inc=1, device_id=friend, device_id_type=MESH)

    loads = [
        pltpu.make_async_copy(src, dst, load_sem.at[n])
        for n, (src, dst) in enumerate(
            ((chosen_in, chosen), (slot_weight_in, slot_weight), (tokens, tok_buf), (out_grad, grad_buf))
        )
    ]
    weights = []
    for n, (src, dst) in enumerate(((w_gate, wg), (w_up, wu), (w_down, wd))):
        middle = dst.shape[0] // 2
        for h in range(2):
            part = pl.ds(h * middle, middle)
            weights.append(pltpu.make_async_copy(src.at[0, part], dst.at[part], w_sem.at[2 * n + h]))
    for copy in loads:
        copy.start()
    loads[0].wait()
    route_picks(me, dp, chosen, pick)
    loads[2].wait()
    rows_in[...] = dot(pick[...], tok_buf[...], NN).astype(BF)
    pl.semaphore_wait(barrier, len(friends))

    block = lambda n: pl.ds(MOST * n, MOST)

    def dispatch(which, g, src, dst):
        return [
            send(src.at[block(n)], dst.at[block(4 * g + n)], disp_s.at[which, 4 * g + n],
                 disp_r.at[which, 4 * g + n], (near_group if g else group)[n])
            for n in (2, 3, 1, 0) if g or n
        ]

    row_copies = [dispatch(0, 0, rows_in, rows)]
    rows[0:MOST, :] = rows_in[0:MOST, :]
    loads[1].wait()
    route_weights(me, dp, near, chosen, slot_weight, weight)
    loads[3].wait()
    for copy in weights:
        copy.start()
    grads_in[...] = dot(pick[...], grad_buf[...], NN).astype(BF)
    grad_copies = [dispatch(1, 0, grads_in, raw)]
    raw[0:MOST, :] = grads_in[0:MOST, :]

    half = rows.shape[1] // 2
    mine = pl.ds(pl.multiple_of(yl * half, half), half)
    slot = lambda d, g: pl.ds(2 * SLOTS * d + SLOTS * g, SLOTS)
    gap = jnp.zeros((SLOTS, 4), BF)
    blank = jnp.zeros((SLOTS, QPAD - QUARTER), BF)
    x_copies, g_copies, late_h, late_gu = [], [], [], []

    def early_sends(which, g, src, dst, reach):
        return [
            send(src, dst.at[slot(n, g)], early_s.at[which, 4 * g + n], early_r.at[which, 4 * g + n], ring_a[n])
            for n in reach
        ]

    def early_forward(which, g, copies, dst):
        for copy in copies:
            copy.wait_recv()
        middle = SLOTS // 2
        forwards = []
        for h, n in ((0, 1), (1, 3)):
            there = lambda d: pl.ds(2 * SLOTS * d + SLOTS * g + middle * h, middle)
            forwards.append(send(
                dst.at[there(n)], dst.at[there(2)], early_s.at[which, 4 * g + 2 * h],
                early_r.at[which, 4 * g + 2 * h], ring_a[n],
            ))
        return forwards

    def late_sends(which, g, src, dst):
        here = pl.ds(SLOTS * g, SLOTS)
        dst[here, :] = src[a, here, :]
        return [
            send(src.at[(a + n) % 4, here], dst.at[slot(n, g)], late_s.at[which, 4 * g + n],
                 late_r.at[which, 4 * g + n], ring_a[n])
            for n in (2, 1, 3)
        ]

    for g in range(2):
        here = pl.ds(SLOTS * g, SLOTS)
        for copy in row_copies[g]:
            copy.wait_recv()
        for which in range(4):
            @pl.when(2 * core + yl == which)
            def _():
                order = [u if which < 2 else 4 * (u % 4) + u // 4 for u in range(16)]
                first = 64 * (which % 2)
                rx[here, :] = jnp.concatenate(
                    [rows[here, 128 * u + first : 128 * u + first + 64] for u in order], axis=1
                )
        x_copies.append(early_sends(0, g, rx.at[here], rx, (1, 3) if g else (2, 1, 3)))
        if g == 0:
            row_copies.append(dispatch(0, 1, rows_in, rows))

        if g == 0:
            for copy in weights[0:4]:
                copy.wait()
        gate_pre = dot(rows[here, :], wg[...], NN)
        up_pre = dot(rows[here, :], wu[...], NN)
        sig = 1.0 / (1.0 + jnp.exp(-gate_pre))
        activated = gate_pre * sig
        ggp[here, :] = (activated * up_pre).astype(BF)
        for which in range(2):
            @pl.when(core == which)
            def _():
                for j in range(4):
                    pieces = []
                    for v in range(8):
                        owner = (v // 2) * 8 + 2 * j + v % 2 if which == 0 else 8 * j + v
                        pieces += [ggp[here, 44 * owner : 44 * owner + 44], gap]
                    hq[j, here, :] = jnp.concatenate(pieces, axis=1)
        late_h += late_sends(0, g, hq, rh)

        for copy in grad_copies[g]:
            copy.wait_recv()
        gout[here, :] = (weight[here, 0:1] * raw[here, :].astype(F32)).astype(BF)
        rg[here, :] = gout[here, mine]
        g_copies.append(early_sends(1, g, rg.at[here], rg, (2, 1, 3) if g else (1, 3)))
        if g == 0:
            grad_copies.append(dispatch(1, 1, grads_in, raw))
        if g == 0:
            for copy in weights[4:6]:
                copy.wait()
        grad_hidden = dot(gout[here, :], wd[...], NT)
        gup[here, :] = (grad_hidden * activated).astype(BF)
        ggp[here, :] = (grad_hidden * up_pre * (sig * (1.0 + gate_pre * (1.0 - sig)))).astype(BF)
        for j in range(4):
            columns = slice(QUARTER * j, QUARTER * (j + 1))
            gq[j, here, :] = jnp.concatenate([gup[here, columns], blank, ggp[here, columns], blank], axis=1)
        late_gu += late_sends(1, g, gq, rgu)

    early_g = early_forward(1, 0, g_copies[0], rg) + g_copies[1]
    early_x = x_copies[0] + early_forward(0, 1, x_copies[1], rx)

    slot_grad = dot(ggp[0:SLOTS, :], wg[...], NT) + dot(gup[0:SLOTS, :], wu[...], NT)
    slot_send[...] = slot_grad.astype(BF)
    returns = [
        send(slot_send.at[block(n)], back.at[block(n)], ret_s.at[n], ret_r.at[n], (dp, (me + 4 - n) % 4))
        for n in (2, 1, 3)
    ]
    back[0:MOST, :] = slot_send[0:MOST, :]

    chunk = half // 4
    rows_d = QPAD // 4

    def far_sends(part, first, second, dst):
        return [
            send(first, dst.at[0], sum_s.at[part, 0], sum_r.at[part, 0], ring_b[1]),
            send(second, dst.at[1], sum_s.at[part, 2], sum_r.at[part, 2], ring_b[3]),
        ]

    def near_sends(part, after, before, dst):
        return [
            send(after, dst.at[0], sum_s.at[part, 1], sum_r.at[part, 1], ring_b[1]),
            send(before, dst.at[1], sum_s.at[part, 3], sum_r.at[part, 3], ring_b[3]),
        ]

    def tile_gu(part, n):
        columns = pl.ds(pl.multiple_of((b + n) % 4 * chunk, chunk), chunk)
        part_gu[part - 1, n] = dot(rx[:, columns], rgu[:, QPAD * (part - 1) : QPAD * part], TN).astype(BF)

    def rows_at(n, h):
        step = rows_d // 2
        return pl.ds(pl.multiple_of((b + n) % 4 * rows_d, rows_d) + h * step, step)

    for copy in early_g + late_h:
        copy.wait_recv()
    part_d[...] = dot(rh[...], rg[...], TN).astype(BF)
    relays = [far_sends(0, part_d.at[rows_at(2, 0)], part_d.at[rows_at(2, 1)], via_d)]
    for copy in early_x + late_gu:
        copy.wait_recv()
    middle = chunk // 2
    for part in (1, 2):
        tile_gu(part, 2)
        far = part_gu.at[part - 1, 2]
        relays.append(far_sends(part, far.at[0:middle], far.at[middle:chunk], via_gu.at[part - 1]))
    tile_gu(1, 1)
    tile_gu(1, 3)
    sums = []
    for copy in relays[0]:
        copy.wait_recv()
    for n, h in ((1, 0), (3, 1)):
        part_d[rows_at(n, h), :] = (part_d[rows_at(n, h), :].astype(F32) + via_d[h].astype(F32)).astype(BF)
    whole = lambda n: pl.ds(pl.multiple_of((b + n) % 4 * rows_d, rows_d), rows_d)
    sums.append(near_sends(0, part_d.at[whole(1)], part_d.at[whole(3)], got_d))
    tile_gu(2, 1)
    tile_gu(2, 3)
    for part in (1, 2):
        for copy in relays[part]:
            copy.wait_recv()
        for n, h in ((1, 0), (3, 1)):
            rows_h = pl.ds(middle * h, middle)
            part_gu[part - 1, n, rows_h, :] = (
                part_gu[part - 1, n, rows_h, :].astype(F32) + via_gu[part - 1, h].astype(F32)
            ).astype(BF)
        sums.append(near_sends(part, part_gu.at[part - 1, 1], part_gu.at[part - 1, 3], got_gu.at[part - 1]))
    tile_gu(1, 0)
    tile_gu(2, 0)

    scale = 1.0 / 32
    for copy in sums[0]:
        copy.wait_recv()
    total = part_d[pl.ds(pl.multiple_of(b * rows_d, rows_d), rows_d), :].astype(F32)
    for n in range(2):
        total = total + got_d[n].astype(F32)
    out_d[...] = (total * scale).astype(BF).reshape(out_d.shape)
    put_d = send(out_d.at[1 - yl], land_d.at[yl], put_s.at[0, 0], put_r.at[0, 0], across)
    land_d[yl] = out_d[yl]
    for part in (1, 2):
        for copy in sums[part]:
            copy.wait_recv()
        total = part_gu[part - 1, 0].astype(F32)
        for n in range(2):
            total = total + got_gu[part - 1, n].astype(F32)
        out_gu[part - 1] = (total * scale).astype(BF).reshape(out_gu.shape[1:])
        for n in (2, 1, 3):
            send(out_gu.at[part - 1, (a + n) % 4], land_gu.at[part - 1, a], put_s.at[part, n],
                 put_r.at[part, n], ring_a[n])
        land_gu[part - 1, a] = out_gu[part - 1, a]

    for copy in started[:-7]:
        copy.wait_send()
    for copy in returns:
        copy.wait_recv()
    for n in range(4):
        part = pl.ds(128 * n, 128)
        token_grad[part, :] = dot(pick[:, part], back[...], TN).astype(BF)
    pltpu.make_async_copy(land_d.at[1 - yl], land_d.at[1 - yl], put_r.at[0, 0]).wait()
    for y in range(2):
        grad_down[0, :, half * y : half * (y + 1)] = land_d[y, 0:44, :]
    for part, dst in ((1, grad_up), (2, grad_gate)):
        for n in (1, 2, 3):
            there = land_gu.at[part - 1, (a + 4 - n) % 4]
            pltpu.make_async_copy(there, there, put_r.at[part, n]).wait()
        for j in range(4):
            dst[0, :, QUARTER * j : QUARTER * (j + 1)] = land_gu[part - 1, j, :, 0:QUARTER]
    for copy in started[-7:]:
        copy.wait_send()


def main_pass(chosen, slot_weight, tokens, out_grad, w_gate, w_up, w_down):
    width = tokens.shape[1]
    hid = w_gate.shape[2]
    half = width // 2
    chunk = half // 4
    vmem = pl.BlockSpec(memory_space=pltpu.VMEM)
    hbm = pl.BlockSpec(memory_space=pl.ANY)
    dma = pltpu.SemaphoreType.DMA

    def buf(*shape):
        return pltpu.VMEM(shape, BF)

    return pl.pallas_call(
        main_kernel,
        out_shape=(
            pltpu.VMEM(tokens.shape, BF),
            pltpu.VMEM((1, width // 32, hid), BF),
            pltpu.VMEM((1, width // 32, hid), BF),
            pltpu.VMEM((1, hid // 32, width), BF),
        ),
        in_specs=[hbm] * 7,
        out_specs=(vmem,) * 4,
        scratch_shapes=[
            pltpu.VMEM(chosen.shape, jnp.int32), pltpu.VMEM(slot_weight.shape, F32),
            buf(SLOTS, tokens.shape[0]),
            buf(*tokens.shape), buf(*tokens.shape),
            pltpu.VMEM((2 * SLOTS, 128), F32),
            buf(SLOTS, width), buf(SLOTS, width),
            buf(width, hid), buf(width, hid), buf(hid, width),
            buf(2 * SLOTS, width), buf(2 * SLOTS, width), buf(2 * SLOTS, width),
            buf(8 * SLOTS, half), buf(8 * SLOTS, half),
            buf(8 * SLOTS, QPAD), buf(8 * SLOTS, 2 * QPAD),
            buf(4, 2 * SLOTS, QPAD), buf(4, 2 * SLOTS, 2 * QPAD),
            buf(2 * SLOTS, hid), buf(2 * SLOTS, hid),
            buf(SLOTS, width), buf(SLOTS, width),
            buf(QPAD, half), buf(2, QPAD // 8, half), buf(2, QPAD // 4, half),
            buf(2, 4, chunk, QPAD), buf(2, 2, chunk // 2, QPAD), buf(2, 2, chunk, QPAD),
            buf(2, 48, half), buf(2, 4, 64, QPAD),
            buf(2, 48, half), buf(2, 4, 64, QPAD),
            dma((4,)), dma((6,)),
            dma((2, 8)), dma((2, 8)),
            dma((2, 8)), dma((2, 8)),
            dma((2, 8)), dma((2, 8)),
            dma((4,)), dma((4,)),
            dma((3, 4)), dma((3, 4)),
            dma((3, 4)), dma((3, 4)),
        ],
        compiler_params=pltpu.CompilerParams(
            collective_id=0, has_side_effects=True, vmem_limit_bytes=56 * 2**20
        ),
    )(chosen, slot_weight, tokens, out_grad, w_gate, w_up, w_down)


def store_kernel(*refs):
    sources, results, sems = refs[0:4], refs[4:8], refs[8]
    pieces = 4
    size = sources[0].shape[0] // pieces
    copies = [pltpu.make_async_copy(sources[n], results[n], sems.at[n]) for n in range(1, 4)]
    for k in range(pieces):
        part = pl.ds(size * k, size)
        copies.append(pltpu.make_async_copy(sources[0].at[part], results[0].at[part], sems.at[4 + k]))
    for copy in copies:
        copy.start()
    for copy in copies:
        copy.wait()


def local(tokens, out_grad, chosen, slot_weight, w_gate, w_up, w_down):
    results = main_pass(chosen, slot_weight, tokens, out_grad, w_gate, w_up, w_down)
    return pl.pallas_call(
        store_kernel,
        out_shape=tuple(jax.ShapeDtypeStruct(value.shape, value.dtype) for value in results),
        in_specs=[pl.BlockSpec(memory_space=pltpu.VMEM)] * 4,
        out_specs=(pl.BlockSpec(memory_space=pl.ANY),) * 4,
        scratch_shapes=[pltpu.SemaphoreType.DMA((8,))],
        compiler_params=pltpu.CompilerParams(vmem_limit_bytes=4 * 2**20),
    )(*results)


def solution(mesh):
    return jax.shard_map(
        local,
        mesh=mesh,
        in_specs=(
            P(("dp", "expert"), None),
            P(("dp", "expert"), None),
            P(),
            P("expert", None),
            P("expert", None, None),
            P("expert", None, None),
            P("expert", None, None),
        ),
        out_specs=(
            P(("dp", "expert"), None),
            P("expert", "dp", None),
            P("expert", "dp", None),
            P("expert", "dp", None),
        ),
        check_vma=False,
    )
```
